32 devices in a mesh: dp: 8 (over z, y), item: 4 (over x, core).
Axes of the slice: x: 2, y: 2, z: 4, core: 2. Of those that a mesh axis runs over, the one named last changes fastest.
Arguments:
- table: bfloat16 [8192, 1024], P('item'), may hold values from -0.5 to 0.5
- w_uvqk: bfloat16 [1024, 4, 1024], P(None, None, 'item'), may hold values from -0.1875 to 0.1875
- w_out: bfloat16 [1024, 1024], P('item'), may hold values from -0.1875 to 0.1875
- history: int32 [8, 1024], P('dp'), may hold values from 0 to 8191
- lengths: int32 [8], P('dp'), may hold values from 1 to 1024, 4096 in all
- candidates: int32 [8, 512], P('dp'), may hold values from 0 to 8191
- counts: int32 [8], P('dp'), may hold values from 128 to 512, as said below
- actions: int32 [8, 1024], P('dp'), may hold values from 0 to 511, as said below
- targets: float32 [8, 1024], P('dp'), may hold values from -6 to 6
Outputs:
- loss: float32 [], replicated
- grad_uvqk: float32 [1024, 4, 1024], P('dp', None, 'item')
- grad_out: float32 [1024, 1024], P('item', 'dp')
- grad_table: float32 [8192, 1024], P('item', 'dp')
The draws below stay inside these ranges and needn't reach their ends.
Inputs may be any that keep to these rules, and one draw needn't show every extreme that they name: `counts`: every user has at least 128 live candidates and some user has all 512. `actions`: each action is below its user's count.
All inputs are finite; a program needn't handle non-finite values. No bound on the sum of `lengths` on one device may be relied on, other than what follows from the above.
Results may differ from the reference program's by a relative error of at most 0.023.
Values may be sent and summed in bfloat16 or wider, within the bound.
A program may use at most 128 MiB of HBM per device.

```python
import math
import jax
import jax.numpy as jnp
import numpy as np
from jax import lax

D = 1024
HEADS = 8
HD = 128
SEQ = 1024
CAND = 512
USERS = 8
ITEMS = 8192
N_DP = 8
N_ITEM = 4


def shared_counts(key):
    lower = jax.random.randint(jax.random.fold_in(key, 11), (USERS,), CAND // 4, CAND + 1)
    chosen = jax.random.randint(jax.random.fold_in(key, 12), (), 0, USERS)
    return jnp.where(jnp.arange(USERS) == chosen, CAND, lower).astype(jnp.int32)


def draw_counts(key, part):
    return shared_counts(key)


def draw_actions(key, part):
    counts = shared_counts(key)
    key = jax.random.fold_in(key, 5)
    raw = jax.random.randint(key, (USERS, SEQ), 0, 1 << 20)
    return (raw % counts[:, None]).astype(jnp.int32)


def draw_table(key, part):
    key = jax.random.fold_in(key, 7)
    values = 0.05 * jax.random.normal(jax.random.fold_in(key, 1), (ITEMS, D), jnp.float32)
    return jnp.clip(values, -0.3, 0.3).astype(jnp.bfloat16)


def plant(result, rng, least, top_value):
    extent = result.shape
    spot = [jax.random.randint(jax.random.fold_in(rng, axis), (), 0, extent[axis]) for axis in range(len(extent))]
    result = result.at[tuple(spot)].set(least)
    longest = extent.index(max(extent))
    spot[longest] = (spot[longest] + 1) % extent[longest]
    return result.at[tuple(spot)].set(top_value)


def shard_levels(key, dims, shards, least, largest):
    factor_of, own = 1.0, jax.random.fold_in(key, 6)
    for dim, parts in shards:
        draws = jnp.exp(jax.random.uniform(jax.random.fold_in(own, dim), (parts,), jnp.float32, least / len(shards), largest / len(shards)))
        factor_of = factor_of * jnp.repeat(draws, dims[dim] // parts).reshape([-1 if axis == dim else 1 for axis in range(len(dims))])
    return factor_of


def rank_bounds(number_of, lean):
    weights = [(1 << 20) // math.isqrt(standing ** lean) + 1 for standing in range(1, number_of + 1)]
    scale = 1 + sum(weights) // (1 << 30)
    return np.cumsum(np.array([max(1, weight // scale) for weight in weights]))


def ranked(own_key, shape, amount, slope):
    grid = rank_bounds(amount, slope)
    pick = jax.random.randint(jax.random.fold_in(own_key, 1), shape, 0, int(grid[amount - 1]))
    standing = jnp.searchsorted(jnp.asarray(grid, jnp.int32), pick, side="right")
    return jax.random.permutation(jax.random.fold_in(own_key, 2), amount)[standing].astype(jnp.int32)


def split_up(amount, total, reach, skew):
    loads = [(1 << 20) // math.isqrt(grade ** skew) + 1 for grade in range(2, amount + 1)]
    rest, holding = total - reach - (amount - 1), [1] * (amount - 1)
    while rest > 0:
        movable = [i for i in range(amount - 1) if holding[i] < reach]
        mass, remaining = sum([loads[i] for i in movable]), rest
        for i in movable:
            more = min(reach - holding[i], max(1, remaining * loads[i] // mass), rest)
            holding[i] = holding[i] + more
            rest = rest - more
    return np.array([reach] + holding)


def ragged(rng, number_of, total, most, slope):
    if number_of == 2:
        one = jax.random.randint(rng, (), max(1, total - most), min(most, total - 1) + 1)
        return jnp.stack([one, total - one])
    sizes = jnp.asarray(split_up(number_of, total, most, slope), jnp.int32)
    twos = (number_of - 1) // 2
    giver, sink = sizes[1:1 + 2 * twos:2], sizes[2:2 + 2 * twos:2]
    slack = jnp.minimum(giver - 1, most - sink)
    moved = jax.random.randint(jax.random.fold_in(rng, 1), (twos,), 0, 1 << 20) % (slack + 1)
    sizes = sizes.at[1:1 + 2 * twos:2].set(giver - moved).at[2:2 + 2 * twos:2].set(sink + moved)
    return sizes[jax.random.permutation(jax.random.fold_in(rng, 2), number_of)]


def bell_draw(rng, extent, width, most, cuts=(), held_as=jnp.bfloat16):
    entries = jax.random.normal(rng, extent, jnp.float32) * width
    if len(cuts) > 0:
        entries = shard_levels(rng, extent, cuts, -0.22, 0.18) * entries
    return jnp.clip(entries, min=-most, max=most).astype(held_as)


def setup_inputs(seed: int = 0) -> dict:
    key_list = jax.random.split(jax.random.key(seed), 10)
    table = draw_table(jax.random.fold_in(key_list[9], 71), 0)
    w_uvqk = bell_draw(key_list[1], (D, 4, D), D ** -0.5, 0.1875, ((2, 4),))
    w_out = bell_draw(key_list[2], (D, D), D ** -0.5, 0.1875, ((0, 4),))
    history = plant(ranked(key_list[3], (USERS, SEQ), ITEMS, 2), jax.random.fold_in(key_list[3], 3), 0, ITEMS - 1).astype(jnp.int32)
    lengths = ragged(key_list[4], USERS, N_DP * SEQ // 2, SEQ, 2).astype(jnp.int32)
    candidates = plant(jax.random.randint(key_list[5], (USERS, CAND), 0, ITEMS), jax.random.fold_in(key_list[5], 1), 0, ITEMS - 1).astype(jnp.int32)
    counts = draw_counts(jax.random.fold_in(key_list[9], 71), 0)
    actions = draw_actions(jax.random.fold_in(key_list[9], 71), 0)
    targets = bell_draw(key_list[8], (USERS, SEQ), 1.0, 6.0, ((0, 8),), jnp.float32)
    return {"table": table, "w_uvqk": w_uvqk, "w_out": w_out, "history": history, "lengths": lengths, "candidates": candidates, "counts": counts, "actions": actions, "targets": targets}


CQL_WEIGHT = 0.5

def silu_slope(value):
    sigma = jax.nn.sigmoid(value)
    return sigma * (1.0 + value * (1.0 - sigma))

def rounded(value):
    return lax.optimization_barrier(value.astype(jnp.bfloat16)).astype(jnp.float32)

def one_user(table, w_uvqk, w_out, hist, length, cand, count, action, target):
    rows = jnp.take(table, hist, axis=0)
    rows_f = rows.astype(jnp.float32)
    scale = lax.rsqrt(lax.optimization_barrier(jnp.mean(rows_f * rows_f, axis=-1, keepdims=True)) + 1e-06)
    normed_f = rows_f * scale
    normed = normed_f.astype(jnp.bfloat16)
    flat_w = w_uvqk.reshape(D, 4 * D)
    pre = jnp.dot(normed, flat_w, preferred_element_type=jnp.float32)
    act = rounded(jax.nn.silu(pre)).reshape(SEQ, 4, HEADS, HD)
    gate_u, values, queries, keys = (act[:, 0], act[:, 1], act[:, 2], act[:, 3])
    places = jnp.arange(SEQ, dtype=jnp.int32)
    allowed = (places[None, :] <= places[:, None]) & (places[None, :] < length)
    weight = allowed.astype(jnp.float32) / length.astype(jnp.float32)
    logits = jnp.einsum('thd,shd->hts', queries, keys) * HD ** (-0.5)
    attn = rounded(jax.nn.silu(logits) * weight)
    mixed = jnp.einsum('hts,shd->thd', attn, values).reshape(SEQ, D)
    center = lax.optimization_barrier(jnp.mean(mixed, axis=-1, keepdims=True))
    rstd = lax.rsqrt(lax.optimization_barrier(jnp.mean(mixed * mixed, axis=-1, keepdims=True)) - center * center + 1e-05)
    normo = (mixed - center) * rstd
    u_flat = gate_u.reshape(SEQ, D)
    gated = (normo * u_flat).astype(jnp.bfloat16)
    hidden = (rows_f + jnp.dot(gated, w_out, preferred_element_type=jnp.float32)).astype(jnp.bfloat16)
    crows = jnp.take(table, cand, axis=0)
    scores = jnp.dot(hidden, crows.T, preferred_element_type=jnp.float32)
    slots = jnp.arange(CAND, dtype=jnp.int32)
    valid = slots[None, :] < count
    masked = jnp.where(valid, scores, -jnp.inf)
    top = lax.optimization_barrier(jnp.max(masked, axis=-1, keepdims=True))
    expo = jnp.exp(masked - top)
    total = lax.optimization_barrier(jnp.sum(expo, axis=-1, keepdims=True))
    lse = top[:, 0] + jnp.log(total[:, 0])
    soft = expo / total
    onehot = (slots[None, :] == action[:, None]).astype(jnp.float32)
    taken = lax.optimization_barrier(jnp.sum(scores * onehot, axis=-1))
    live = (places < length).astype(jnp.float32) / SEQ
    miss = taken - target
    loss = jnp.sum(live * (CQL_WEIGHT * (lse - taken) + 0.5 * miss * miss))
    dscore = rounded(live[:, None] * (CQL_WEIGHT * soft + (miss - CQL_WEIGHT)[:, None] * onehot))
    dhidden = rounded(jnp.dot(dscore, crows.astype(jnp.float32)))
    block = SEQ // N_ITEM
    pieces = jnp.einsum('nbc,nbd->ncd', dscore.reshape(N_ITEM, block, CAND), hidden.astype(jnp.float32).reshape(N_ITEM, block, D))
    dcand = lax.optimization_barrier(jnp.sum(rounded(pieces), axis=0))
    out_f = w_out.astype(jnp.float32)
    dgated = jnp.dot(dhidden, out_f.T)
    grad_out = jnp.dot(gated.astype(jnp.float32).T, dhidden)
    du = dgated * normo
    dnormo = dgated * u_flat
    first = lax.optimization_barrier(jnp.mean(dnormo, axis=-1, keepdims=True))
    second = lax.optimization_barrier(jnp.mean(dnormo * normo, axis=-1, keepdims=True))
    dmixed = rounded(rstd * (dnormo - first - normo * second)).reshape(SEQ, HEADS, HD)
    dattn = jnp.einsum('thd,shd->hts', dmixed, values)
    dvalues = jnp.einsum('hts,thd->shd', attn, dmixed)
    dlogits = rounded(dattn * weight * silu_slope(logits) * HD ** (-0.5))
    dqueries = jnp.einsum('hts,shd->thd', dlogits, keys)
    dkeys = jnp.einsum('hts,thd->shd', dlogits, queries)
    dact = jnp.stack([du.reshape(SEQ, HEADS, HD), dvalues, dqueries, dkeys], axis=1).reshape(SEQ, 4 * D)
    dpre = (dact * silu_slope(pre)).astype(jnp.bfloat16)
    grad_in = jnp.dot(normed.T, dpre, preferred_element_type=jnp.float32)
    group = HEADS // N_ITEM * HD
    dgroups = jnp.einsum('skne,dkne->nsd', dpre.astype(jnp.float32).reshape(SEQ, 4, N_ITEM, group), w_uvqk.astype(jnp.float32).reshape(D, 4, N_ITEM, group))
    dnormed = lax.optimization_barrier(jnp.sum(rounded(dgroups), axis=0))
    drows = dhidden + scale * (dnormed - normed_f * lax.optimization_barrier(jnp.mean(dnormed * normed_f, axis=-1, keepdims=True)))
    return (loss, grad_in.reshape(D, 4, D), grad_out, drows, dcand)

def reference(table, w_uvqk, w_out, history, lengths, candidates, counts, actions, targets):

    def advance(carry, user):
        loss, grad_in, grad_out, grad_table = carry
        hist, length, cand, count, action, target = user
        terms = one_user(table, w_uvqk, w_out, hist, length, cand, count, action, target)
        grad_table = grad_table.at[hist].add(terms[3]).at[cand].add(terms[4])
        return ((loss + terms[0], grad_in + terms[1], grad_out + terms[2], grad_table), None)
    start = (jnp.zeros((), jnp.float32), jnp.zeros((D, 4, D), jnp.float32), jnp.zeros((D, D), jnp.float32), jnp.zeros((ITEMS, D), jnp.float32))
    final, unused = lax.scan(advance, start, (history, lengths, candidates, counts, actions, targets))
    return (final[0], final[1], final[2], final[3])
```

```python
import jax
import jax.numpy as jnp
from jax import lax
from jax.experimental import pallas as pl
from jax.experimental.pallas import tpu as pltpu
from jax.sharding import PartitionSpec as P

HD = 128


CQL_WEIGHT = 0.5
MESH = pl.DeviceIdType.MESH
VMEM = pl.BlockSpec(memory_space=pltpu.VMEM)


def silu_slope(value):
    sigma = jax.nn.sigmoid(value)
    return sigma * (1.0 + value * (1.0 - sigma))


def spot(axis):
    me = lax.axis_index(axis)
    return me // 2, me % 2


def meet(peers):
    barrier = pltpu.get_barrier_semaphore()
    for peer in peers:
        pl.semaphore_signal(barrier, inc=1, device_id=peer, device_id_type=MESH)
    pl.semaphore_wait(barrier, len(peers))


def near(axis):
    pairs = lax.axis_size(axis) // 2
    outer, inner = spot(axis)
    other = {axis: outer * 2 + 1 - inner}
    far = [{axis: lax.rem(outer + k, pairs) * 2 + inner} for k in range(1, pairs)]
    return other, far


def send(src, dst, sems, index, peer):
    copy = pltpu.make_async_remote_copy(
        src_ref=src,
        dst_ref=dst,
        send_sem=sems[0].at[index],
        recv_sem=sems[1].at[index],
        device_id=peer,
        device_id_type=MESH,
    )
    copy.start()
    return copy


def sem_pair(*shape):
    return [pltpu.SemaphoreType.DMA(shape), pltpu.SemaphoreType.DMA(shape)]


def params(number):
    return pltpu.CompilerParams(
        collective_id=number, has_side_effects=True, vmem_limit_bytes=40 * 1024 * 1024
    )


def join_kernel(pairs, pieces, in_ref, out_ref, got, mine, far_got, s1, r1, s2, r2, s3, r3):
    outer, inner = spot("item")
    other, far = near("item")
    meet([other] + far)
    first = [
        send(in_ref.at[1 - inner, p], got.at[p], (s1, r1), p, other) for p in range(pieces)
    ]
    second = []
    for p in range(pieces):
        first[p].wait_recv()
        mine[p] = in_ref[inner, p] + got[p]
        for k in range(1, pairs):
            second.append(
                send(mine.at[p], far_got.at[k - 1, p], (s2, r2), (k - 1) * pieces + p, far[k - 1])
            )
    third = []
    for p in range(pieces):
        total = mine[p]
        for k in range(1, pairs):
            second[p * (pairs - 1) + k - 1].wait_recv()
            total = total + far_got[k - 1, p]
        out_ref[inner, p] = total
        third.append(send(out_ref.at[inner, p], out_ref.at[inner, p], (s3, r3), p, other))
    for copy in third:
        copy.wait_recv()
    for copy in first + second + third:
        copy.wait_send()


def join(array, number, pieces):
    pairs = lax.axis_size("item") // 2
    rows, width = array.shape
    block = rows // 2 // pieces
    spread = (max(pairs - 1, 1) * pieces,)
    out = pl.pallas_call(
        lambda *refs: join_kernel(pairs, pieces, *refs),
        out_shape=jax.ShapeDtypeStruct((2, pieces, block, width), array.dtype),
        in_specs=[VMEM],
        out_specs=VMEM,
        scratch_shapes=[
            pltpu.VMEM((pieces, block, width), array.dtype),
            pltpu.VMEM((pieces, block, width), array.dtype),
            pltpu.VMEM((max(pairs - 1, 1), pieces, block, width), array.dtype),
            *sem_pair(pieces),
            *sem_pair(*spread),
            *sem_pair(pieces),
        ],
        compiler_params=params(number),
        name="join_rows",
    )(array.reshape(2, pieces, block, width))
    return out.reshape(rows, width)


def tally_kernel(count, in_ref, out_ref, got, ss, rs):
    me = lax.axis_index("item")
    peers = [{"item": lax.rem(me + k, count)} for k in range(1, count)]
    meet(peers)
    copies = [send(in_ref, got.at[k], (ss, rs), k, peer) for k, peer in enumerate(peers)]
    total = in_ref[...]
    for k in range(count - 1):
        copies[k].wait_recv()
        total = total + got[k]
    out_ref[...] = total
    for copy in copies:
        copy.wait_send()


def tally(first, second, number):
    count = lax.axis_size("item")
    size = first.shape[0]
    packed = jnp.stack([first, second]).reshape(2 * size // 128, 128)
    out = pl.pallas_call(
        lambda *refs: tally_kernel(count, *refs),
        out_shape=jax.ShapeDtypeStruct(packed.shape, packed.dtype),
        in_specs=[VMEM],
        out_specs=VMEM,
        scratch_shapes=[
            pltpu.VMEM((count - 1, *packed.shape), packed.dtype),
            *sem_pair(count - 1),
        ],
        compiler_params=params(number),
        name="tally",
    )(packed)
    out = out.reshape(2, size)
    return out[0], out[1]


def reduce_kernel(plan, *refs):
    n = len(plan)
    ins, outs = refs[:n], refs[n : 2 * n]
    work = [refs[2 * n + 7 * i : 2 * n + 7 * i + 7] for i in range(n)]
    axes = sorted({axis for axis, _, _ in plan})
    ties = {axis: near(axis) for axis in axes}
    meet([peer for axis in axes for peer in [ties[axis][0]] + ties[axis][1]])
    first, second = {}, {}
    order = [(i, p) for p in range(max(pieces for _, _, pieces in plan)) for i in range(n) if p < plan[i][2]]
    for i, p in order:
        axis, pairs, pieces = plan[i]
        outer, inner = spot(axis)
        got, mine, far_got, s1, r1, s2, r2 = work[i]
        for k in list(range(1, pairs)) + [0]:
            to = lax.rem(outer + k, pairs)
            first[i, p, k] = send(
                ins[i].at[to, 1 - inner, p], got.at[k, p], (s1, r1), k * pieces + p, ties[axis][0]
            )
    for i, p in order:
        axis, pairs, pieces = plan[i]
        outer, inner = spot(axis)
        got, mine, far_got, s1, r1, s2, r2 = work[i]
        for k in range(1, pairs):
            first[i, p, k].wait_recv()
            to = lax.rem(outer + k, pairs)
            mine[k - 1, p] = (
                ins[i][to, inner, p].astype(jnp.float32) + got[k, p].astype(jnp.float32)
            ).astype(jnp.bfloat16)
            second[i, p, k] = send(
                mine.at[k - 1, p],
                far_got.at[k - 1, p],
                (s2, r2),
                (k - 1) * pieces + p,
                ties[axis][1][k - 1],
            )
    for i, p in order:
        axis, pairs, pieces = plan[i]
        outer, inner = spot(axis)
        got, mine, far_got, s1, r1, s2, r2 = work[i]
        first[i, p, 0].wait_recv()
        total = ins[i][outer, inner, p].astype(jnp.float32) + got[0, p].astype(jnp.float32)
        for k in range(1, pairs):
            second[i, p, k].wait_recv()
            total = total + far_got[k - 1, p].astype(jnp.float32)
        outs[i][p] = total
    for copy in list(first.values()) + list(second.values()):
        copy.wait_send()


def reduce_parts(items, number):
    plan, arrays, shapes, scratch = [], [], [], []
    for axis, array, pieces in items:
        count, rows, width = array.shape
        pairs, block = count // 2, rows // pieces
        plan.append((axis, pairs, pieces))
        arrays.append(array.reshape(pairs, 2, pieces, block, width))
        shapes.append(jax.ShapeDtypeStruct((pieces, block, width), jnp.float32))
        others = max(pairs - 1, 1)
        scratch += [
            pltpu.VMEM((pairs, pieces, block, width), array.dtype),
            pltpu.VMEM((others, pieces, block, width), array.dtype),
            pltpu.VMEM((others, pieces, block, width), array.dtype),
            *sem_pair(pairs * pieces),
            *sem_pair(others * pieces),
        ]
    outs = pl.pallas_call(
        lambda *refs: reduce_kernel(plan, *refs),
        out_shape=shapes,
        in_specs=[VMEM] * len(plan),
        out_specs=[VMEM] * len(plan),
        scratch_shapes=scratch,
        compiler_params=params(number),
        name="reduce_parts",
    )(*arrays)
    return [out.reshape(-1, out.shape[-1]) for out in outs]


def spread_kernel(pairs, pieces, in_ref, out_ref, local, s1, r1, s2, r2, s3, r3):
    outer, inner = spot("item")
    other, far = near("item")
    meet([other] + far)
    keep = pltpu.make_async_copy(in_ref, out_ref.at[outer, inner], local)
    keep.start()
    away, beside, onward = {}, [], []
    for p in range(pieces):
        for k in range(1, pairs):
            away[p, k] = send(
                in_ref.at[p],
                out_ref.at[outer, inner, p],
                (s1, r1),
                (k - 1) * pieces + p,
                far[k - 1],
            )
    for p in range(pieces):
        beside.append(send(in_ref.at[p], out_ref.at[outer, inner, p], (s2, r2), p, other))
    for p in range(pieces):
        for k in range(1, pairs):
            away[p, k].wait_recv()
            came = lax.rem(outer + pairs - k, pairs)
            onward.append(
                send(
                    out_ref.at[came, inner, p],
                    out_ref.at[came, inner, p],
                    (s3, r3),
                    (k - 1) * pieces + p,
                    other,
                )
            )
    keep.wait()
    for copy in beside + onward:
        copy.wait_recv()
    for copy in list(away.values()) + beside + onward:
        copy.wait_send()


def spread(array, number, pieces):
    pairs = lax.axis_size("item") // 2
    rows, width = array.shape
    others = max(pairs - 1, 1)
    out = pl.pallas_call(
        lambda *refs: spread_kernel(pairs, pieces, *refs),
        out_shape=jax.ShapeDtypeStruct((pairs, 2, pieces, rows // pieces, width), array.dtype),
        in_specs=[VMEM],
        out_specs=VMEM,
        scratch_shapes=[
            pltpu.SemaphoreType.DMA,
            *sem_pair(others * pieces),
            *sem_pair(pieces),
            *sem_pair(others * pieces),
        ],
        compiler_params=params(number),
        name="spread",
    )(array.reshape(pieces, rows // pieces, width))
    return out.reshape(-1, width)


def trade_kernel(pairs, users, in_ref, out_ref, local, s0, r0, s1, r1, s2, r2, s3, r3):
    outer, inner = spot("item")
    me = lax.axis_index("dp")
    other, far = near("item")
    peers = [{"dp": lax.rem(me + k, users)} for k in range(1, users)]
    meet([other] + far + peers)
    here = out_ref.at[outer, inner]
    keep = pltpu.make_async_copy(in_ref.at[me], here.at[me], local)
    keep.start()
    swap, away, beside, onward = {}, {}, [], []
    for k in range(1, users):
        swap[k] = send(in_ref.at[lax.rem(me + k, users)], here.at[me], (s0, r0), k, peers[k - 1])
    for k in range(users):
        if k == 0:
            keep.wait()
        else:
            swap[k].wait_recv()
        user = lax.rem(me + users - k, users)
        for j in range(1, pairs):
            away[k, j] = send(
                here.at[user], here.at[user], (s1, r1), (j - 1) * users + k, far[j - 1]
            )
        beside.append(send(here.at[user], here.at[user], (s2, r2), k, other))
    for k in range(users):
        user = lax.rem(me + users - k, users)
        for j in range(1, pairs):
            away[k, j].wait_recv()
            came = out_ref.at[lax.rem(outer + pairs - j, pairs), inner, user]
            onward.append(send(came, came, (s3, r3), (j - 1) * users + k, other))
    for copy in beside + onward:
        copy.wait_recv()
    for copy in list(swap.values()) + list(away.values()) + beside + onward:
        copy.wait_send()


def trade(array, number):
    pairs = lax.axis_size("item") // 2
    users, rows, width = array.shape
    others = max(pairs - 1, 1)
    return pl.pallas_call(
        lambda *refs: trade_kernel(pairs, users, *refs),
        out_shape=jax.ShapeDtypeStruct((pairs, 2, users, rows, width), array.dtype),
        in_specs=[VMEM],
        out_specs=VMEM,
        scratch_shapes=[
            pltpu.SemaphoreType.DMA,
            *sem_pair(users),
            *sem_pair(others * users),
            *sem_pair(users),
            *sem_pair(others * users),
        ],
        compiler_params=params(number),
        name="trade",
    )(array)


def gather_add_kernel(tile, ids_ref, terms_ref, out_ref):
    @pl.when(pl.program_id(0) == 0)
    def _():
        out_ref[...] = jnp.zeros_like(out_ref)

    ids = ids_ref[...]
    terms = terms_ref[...]

    @pl.loop(0, out_ref.shape[0] // tile)
    def _(step):
        begin = pl.multiple_of(step * tile, tile)
        place = lax.broadcasted_iota(jnp.int32, (tile, ids.shape[1]), 0) + begin
        hit = jnp.where(place == ids, 1.0, 0.0).astype(jnp.bfloat16)
        out_ref[pl.ds(begin, tile), :] += jnp.dot(hit, terms, preferred_element_type=jnp.float32)


def add_rows(ids, terms, rows):
    count, width = terms.shape
    step, tile = 1024, 256
    return pl.pallas_call(
        lambda *refs: gather_add_kernel(tile, *refs),
        out_shape=jax.ShapeDtypeStruct((rows, width), jnp.float32),
        grid=(count // step,),
        in_specs=[
            pl.BlockSpec((1, step), lambda i: (0, i)),
            pl.BlockSpec((step, width), lambda i: (i, 0)),
        ],
        out_specs=pl.BlockSpec((rows, width), lambda i: (0, 0)),
        compiler_params=pltpu.CompilerParams(vmem_limit_bytes=40 * 1024 * 1024),
        name="add_rows",
    )(ids.reshape(1, count), terms)


def on_device(table, w_uvqk, w_out, history, lengths, candidates, counts, actions, targets):
    rows_total = table.shape[0]
    width = table.shape[1]
    seq = history.shape[1]
    ncand = candidates.shape[1]
    parts = lax.axis_size("item")
    block = seq // parts
    owner = lax.axis_index("item")
    first_row = owner * rows_total
    heads_local = w_out.shape[0] // HD

    users = lax.axis_size("dp")
    ids = jnp.concatenate([history[0], candidates[0]]) - first_row
    hit = ids[:, None] == jnp.arange(rows_total, dtype=jnp.int32)[None, :]
    own = jnp.dot(hit.astype(jnp.bfloat16), table, preferred_element_type=jnp.float32)
    joined = join(own.astype(jnp.bfloat16), 0, 8)
    rows_f = joined[:seq].astype(jnp.float32)
    cand_f = joined[seq:]
    all_ids = lax.all_gather(jnp.concatenate([history[0], candidates[0]]), "dp")
    crows = cand_f
    scale = lax.rsqrt(jnp.mean(rows_f * rows_f, axis=-1, keepdims=True) + 1e-06)
    normed_f = rows_f * scale
    normed = normed_f.astype(jnp.bfloat16)
    local_w = w_uvqk.reshape(width, -1)
    pre = jnp.dot(normed, local_w, preferred_element_type=jnp.float32)
    act = jax.nn.silu(pre).astype(jnp.bfloat16).reshape(seq, 4, heads_local, HD)
    gate_u, values, queries, keys = (act[:, 0], act[:, 1], act[:, 2], act[:, 3])
    length = lengths[0]
    places = jnp.arange(seq, dtype=jnp.int32)
    allowed = (places[None, :] <= places[:, None]) & (places[None, :] < length)
    weight = allowed.astype(jnp.float32) / length.astype(jnp.float32)
    logits = jnp.einsum("thd,shd->hts", queries, keys, preferred_element_type=jnp.float32) * HD ** (
        -0.5
    )
    attn = (jax.nn.silu(logits) * weight).astype(jnp.bfloat16)
    mixed = jnp.einsum("hts,shd->thd", attn, values, preferred_element_type=jnp.float32).reshape(
        seq, -1
    )
    sums, squares = tally(jnp.sum(mixed, axis=-1), jnp.sum(mixed * mixed, axis=-1), 1)
    center = (sums / width)[:, None]
    rstd = lax.rsqrt(squares[:, None] / width - center * center + 1e-05)
    normo = (mixed - center) * rstd
    u_flat = gate_u.reshape(seq, -1).astype(jnp.float32)
    gated = (normo * u_flat).astype(jnp.bfloat16)
    out_part = jnp.dot(gated, w_out, preferred_element_type=jnp.float32).astype(jnp.bfloat16)
    out_rows = reduce_parts([("item", out_part.reshape(parts, block, width), 4)], 2)[0]
    begin = owner * block
    rows_block = lax.dynamic_slice_in_dim(rows_f, begin, block, 0)
    hidden = (rows_block + out_rows).astype(jnp.bfloat16)
    scores = jnp.einsum("td,cd->tc", hidden, crows, preferred_element_type=jnp.float32)
    slots = jnp.arange(ncand, dtype=jnp.int32)
    valid = slots[None, :] < counts[0]
    masked = jnp.where(valid, scores, -jnp.inf)
    top = jnp.max(masked, axis=-1, keepdims=True)
    expo = jnp.exp(masked - top)
    total = jnp.sum(expo, axis=-1, keepdims=True)
    lse = top[:, 0] + jnp.log(total[:, 0])
    soft = expo / total
    action_block = lax.dynamic_slice_in_dim(actions[0], begin, block, 0)
    target_block = lax.dynamic_slice_in_dim(targets[0], begin, block, 0)
    onehot = (slots[None, :] == action_block[:, None]).astype(jnp.float32)
    taken = jnp.sum(scores * onehot, axis=-1)
    block_places = begin + jnp.arange(block, dtype=jnp.int32)
    live = (block_places < length).astype(jnp.float32) / seq
    miss = taken - target_block
    loss_part = jnp.sum(live * (CQL_WEIGHT * (lse - taken) + 0.5 * miss * miss))
    dscore = (live[:, None] * (CQL_WEIGHT * soft + (miss - CQL_WEIGHT)[:, None] * onehot)).astype(
        jnp.bfloat16
    )
    dhidden = jnp.dot(dscore, crows, preferred_element_type=jnp.float32).astype(jnp.bfloat16)
    dcand_part = jnp.einsum("tc,td->cd", dscore, hidden, preferred_element_type=jnp.float32).astype(
        jnp.bfloat16
    )
    dh_full = spread(dhidden, 3, 4)
    dgated = jnp.einsum("td,ed->te", dh_full, w_out, preferred_element_type=jnp.float32)
    dw_out = jnp.einsum(
        "te,tdk->dek",
        gated,
        dh_full.reshape(seq, users, width // users),
        preferred_element_type=jnp.float32,
    ).astype(jnp.bfloat16)
    du = dgated * normo
    dnormo = dgated * u_flat
    first_sum, second_sum = tally(
        jnp.sum(dnormo, axis=-1), jnp.sum(dnormo * normo, axis=-1), 4
    )
    first = (first_sum / width)[:, None]
    second = (second_sum / width)[:, None]
    dmixed = (
        (rstd * (dnormo - first - normo * second))
        .astype(jnp.bfloat16)
        .reshape(seq, heads_local, HD)
    )
    dattn = jnp.einsum("thd,shd->hts", dmixed, values, preferred_element_type=jnp.float32)
    dvalues = jnp.einsum("hts,thd->shd", attn, dmixed, preferred_element_type=jnp.float32)
    dlogits = (dattn * weight * silu_slope(logits) * HD ** (-0.5)).astype(jnp.bfloat16)
    dqueries = jnp.einsum("hts,shd->thd", dlogits, keys, preferred_element_type=jnp.float32)
    dkeys = jnp.einsum("hts,thd->shd", dlogits, queries, preferred_element_type=jnp.float32)
    dact = jnp.stack([du.reshape(seq, heads_local, HD), dvalues, dqueries, dkeys], axis=1).reshape(
        seq, -1
    )
    dpre = (dact * silu_slope(pre)).astype(jnp.bfloat16)
    dw_in = jnp.einsum("sd,sk->dk", normed, dpre, preferred_element_type=jnp.float32).astype(
        jnp.bfloat16
    )
    dnormed_part = jnp.einsum(
        "sk,dk->sd", dpre, local_w, preferred_element_type=jnp.float32
    ).astype(jnp.bfloat16)
    cblock = ncand // parts
    dnormed, dcand, grad_in, grad_proj = reduce_parts(
        [
            ("item", dnormed_part.reshape(parts, block, width), 4),
            ("item", dcand_part.reshape(parts, cblock, width), 2),
            ("dp", dw_in.reshape(users, width // users, -1), 2),
            ("dp", dw_out, 1),
        ],
        5,
    )
    grad_in = grad_in.reshape(width // users, 4, -1)
    scale_block = lax.dynamic_slice_in_dim(scale, begin, block, 0)
    normed_block = rows_block * scale_block
    drows = dhidden.astype(jnp.float32) + scale_block * (
        dnormed - normed_block * jnp.mean(dnormed * normed_block, axis=-1, keepdims=True)
    )
    terms = jnp.concatenate([drows, dcand]).astype(jnp.bfloat16)
    terms = terms.reshape(block + cblock, users, width // users).transpose(1, 0, 2)
    traded = trade(terms, 6)
    hist_ids = all_ids[:, :seq].reshape(users, parts, block)
    cand_ids = all_ids[:, seq:].reshape(users, parts, cblock)
    place = jnp.concatenate([hist_ids, cand_ids], axis=2).transpose(1, 0, 2) - first_row
    shard_grad = add_rows(place.reshape(-1), traded.reshape(-1, width // users), rows_total)
    loss = lax.psum(loss_part, ("dp", "item"))
    return (loss, grad_in, grad_proj, shard_grad)


def solution(mesh):
    placed = (
        P("item", None),
        P(None, None, "item"),
        P("item", None),
        P("dp", None),
        P("dp"),
        P("dp", None),
        P("dp"),
        P("dp", None),
        P("dp", None),
    )
    return jax.shard_map(
        on_device,
        mesh=mesh,
        in_specs=placed,
        out_specs=(P(), P("dp", None, "item"), P("item", "dp"), P("item", "dp")),
        check_vma=False,
    )
```

```python
import jax
import jax.numpy as jnp
from jax import lax
from jax.experimental import pallas as pl
from jax.experimental.pallas import tpu as pltpu
from jax.sharding import PartitionSpec as P

HD = 128


CQL_WEIGHT = 0.5
MESH = pl.DeviceIdType.MESH
VMEM = pl.BlockSpec(memory_space=pltpu.VMEM)


def silu_slope(value):
    sigma = jax.nn.sigmoid(value)
    return sigma * (1.0 + value * (1.0 - sigma))


def spot(axis):
    me = lax.axis_index(axis)
    return me // 2, me % 2


def meet(peers):
    barrier = pltpu.get_barrier_semaphore()
    for peer in peers:
        pl.semaphore_signal(barrier, inc=1, device_id=peer, device_id_type=MESH)
    pl.semaphore_wait(barrier, len(peers))


def near(axis):
    pairs = lax.axis_size(axis) // 2
    outer, inner = spot(axis)
    other = {axis: outer * 2 + 1 - inner}
    far = [{axis: lax.rem(outer + k, pairs) * 2 + inner} for k in range(1, pairs)]
    return other, far


def link(src, dst, sems, index, peer):
    return pltpu.make_async_remote_copy(
        src_ref=src,
        dst_ref=dst,
        send_sem=sems[0].at[index],
        recv_sem=sems[1].at[index],
        device_id=peer,
        device_id_type=MESH,
    )


def send(*way):
    copy = link(*way)
    copy.start()
    return copy


def sem_pair(*shape):
    return [pltpu.SemaphoreType.DMA(shape), pltpu.SemaphoreType.DMA(shape)]


def params(number):
    return pltpu.CompilerParams(
        collective_id=number, has_side_effects=True, vmem_limit_bytes=40 * 1024 * 1024
    )


def join_kernel(pairs, pieces, in_ref, out_ref, got, mine, far_got, s1, r1, s2, r2, s3, r3):
    outer, inner = spot("item")
    other, far = near("item")
    meet([other] + far)
    first = [
        send(in_ref.at[1 - inner, p], got.at[p], (s1, r1), p, other) for p in range(pieces)
    ]
    second = []
    for p in range(pieces):
        first[p].wait_recv()
        mine[p] = in_ref[inner, p] + got[p]
        for k in range(1, pairs):
            second.append(
                send(mine.at[p], far_got.at[k - 1, p], (s2, r2), (k - 1) * pieces + p, far[k - 1])
            )
    third = []
    for p in range(pieces):
        total = mine[p]
        for k in range(1, pairs):
            second[p * (pairs - 1) + k - 1].wait_recv()
            total = total + far_got[k - 1, p]
        out_ref[inner, p] = total
        third.append(send(out_ref.at[inner, p], out_ref.at[inner, p], (s3, r3), p, other))
    for copy in third:
        copy.wait_recv()
    for copy in first + second + third:
        copy.wait_send()


def join(array, number, pieces):
    pairs = lax.axis_size("item") // 2
    rows, width = array.shape
    block = rows // 2 // pieces
    spread = (max(pairs - 1, 1) * pieces,)
    out = pl.pallas_call(
        lambda *refs: join_kernel(pairs, pieces, *refs),
        out_shape=jax.ShapeDtypeStruct((2, pieces, block, width), array.dtype),
        in_specs=[VMEM],
        out_specs=VMEM,
        scratch_shapes=[
            pltpu.VMEM((pieces, block, width), array.dtype),
            pltpu.VMEM((pieces, block, width), array.dtype),
            pltpu.VMEM((max(pairs - 1, 1), pieces, block, width), array.dtype),
            *sem_pair(pieces),
            *sem_pair(*spread),
            *sem_pair(pieces),
        ],
        compiler_params=params(number),
        name="join_rows",
    )(array.reshape(2, pieces, block, width))
    return out.reshape(rows, width)


def tally_kernel(count, in_ref, out_ref, got, ss, rs):
    me = lax.axis_index("item")
    peers = [{"item": lax.rem(me + k, count)} for k in range(1, count)]
    meet(peers)
    copies = [send(in_ref, got.at[me], (ss, rs), k, peer) for k, peer in enumerate(peers)]
    got[me] = in_ref[...]
    for copy in copies:
        copy.wait_recv()
    total = got[0]
    for source in range(1, count):
        total = total + got[source]
    out_ref[...] = total
    for copy in copies:
        copy.wait_send()


def tally(packed, number):
    count = lax.axis_size("item")
    return pl.pallas_call(
        lambda *refs: tally_kernel(count, *refs),
        out_shape=jax.ShapeDtypeStruct(packed.shape, packed.dtype),
        in_specs=[VMEM],
        out_specs=VMEM,
        scratch_shapes=[
            pltpu.VMEM((count, *packed.shape), packed.dtype),
            *sem_pair(count - 1),
        ],
        compiler_params=params(number),
        name="tally",
    )(packed)


def pair_sums(mixed, other):
    return jnp.stack([jnp.sum(mixed, axis=-1), jnp.sum(other, axis=-1)]).reshape(-1, 128)


def shift(array, axis, step):
    count = lax.axis_size(axis)
    if step == 0:
        moves = [(i, i ^ 1) for i in range(count)]
    else:
        moves = [(i, (i + 2 * step) % count) for i in range(count)]
    return lax.ppermute(array, axis, moves)


def join_later(array):
    pairs = lax.axis_size("item") // 2
    rows, width = array.shape
    _, inner = spot("item")
    halves = array.reshape(2, rows // 2, width)
    mine = lax.dynamic_index_in_dim(halves, inner, 0, False) + shift(
        lax.dynamic_index_in_dim(halves, 1 - inner, 0, False), "item", 0
    )
    total = mine
    for k in range(1, pairs):
        total = total + shift(mine, "item", k)
    other = shift(total, "item", 0)
    return jnp.where(inner == 0, jnp.stack([total, other]), jnp.stack([other, total])).reshape(
        rows, width
    )


def reduce_later(array):
    count, rows, width = array.shape
    pairs = count // 2
    outer, inner = spot("dp")
    array = array.reshape(pairs, 2, rows, width)
    got = shift(lax.dynamic_index_in_dim(array, 1 - inner, 1, False), "dp", 0)
    mine = (
        lax.dynamic_index_in_dim(array, inner, 1, False).astype(jnp.float32)
        + got.astype(jnp.float32)
    ).astype(jnp.bfloat16)
    total = lax.dynamic_index_in_dim(mine, outer, 0, False).astype(jnp.float32)
    for k in range(1, pairs):
        part = lax.dynamic_index_in_dim(mine, lax.rem(outer + k, pairs), 0, False)
        total = total + shift(part, "dp", k).astype(jnp.float32)
    return total


def reduce_kernel(plan, *refs):
    n = len(plan)
    ins, outs = refs[:n], refs[n : 2 * n]
    work = [refs[2 * n + 7 * i : 2 * n + 7 * i + 7] for i in range(n)]
    axes = sorted({axis for axis, _, _ in plan})
    ties = {axis: near(axis) for axis in axes}
    meet([peer for axis in axes for peer in [ties[axis][0]] + ties[axis][1]])
    first, second = {}, {}
    order = [(i, p) for p in range(max(pieces for _, _, pieces in plan)) for i in range(n) if p < plan[i][2]]
    for i, p in order:
        axis, pairs, pieces = plan[i]
        outer, inner = spot(axis)
        got, mine, far_got, s1, r1, s2, r2 = work[i]
        for k in list(range(1, pairs)) + [0]:
            to = lax.rem(outer + k, pairs)
            first[i, p, k] = send(
                ins[i].at[to, 1 - inner, p], got.at[k, p], (s1, r1), k * pieces + p, ties[axis][0]
            )
    for i, p in order:
        axis, pairs, pieces = plan[i]
        outer, inner = spot(axis)
        got, mine, far_got, s1, r1, s2, r2 = work[i]
        for k in range(1, pairs):
            first[i, p, k].wait_recv()
            to = lax.rem(outer + k, pairs)
            mine[k - 1, p] = (
                ins[i][to, inner, p].astype(jnp.float32) + got[k, p].astype(jnp.float32)
            ).astype(jnp.bfloat16)
            second[i, p, k] = send(
                mine.at[k - 1, p],
                far_got.at[k - 1, p],
                (s2, r2),
                (k - 1) * pieces + p,
                ties[axis][1][k - 1],
            )
    for i, p in order:
        axis, pairs, pieces = plan[i]
        outer, inner = spot(axis)
        got, mine, far_got, s1, r1, s2, r2 = work[i]
        first[i, p, 0].wait_recv()
        total = ins[i][outer, inner, p].astype(jnp.float32) + got[0, p].astype(jnp.float32)
        for k in range(1, pairs):
            second[i, p, k].wait_recv()
            total = total + far_got[k - 1, p].astype(jnp.float32)
        outs[i][p] = total
    for copy in list(first.values()) + list(second.values()):
        copy.wait_send()


def reduce_parts(items, number):
    plan, arrays, shapes, scratch = [], [], [], []
    for axis, array, pieces in items:
        count, rows, width = array.shape
        pairs, block = count // 2, rows // pieces
        plan.append((axis, pairs, pieces))
        arrays.append(array.reshape(pairs, 2, pieces, block, width))
        shapes.append(jax.ShapeDtypeStruct((pieces, block, width), jnp.float32))
        others = max(pairs - 1, 1)
        scratch += [
            pltpu.VMEM((pairs, pieces, block, width), array.dtype),
            pltpu.VMEM((others, pieces, block, width), array.dtype),
            pltpu.VMEM((others, pieces, block, width), array.dtype),
            *sem_pair(pairs * pieces),
            *sem_pair(others * pieces),
        ]
    outs = pl.pallas_call(
        lambda *refs: reduce_kernel(plan, *refs),
        out_shape=shapes,
        in_specs=[VMEM] * len(plan),
        out_specs=[VMEM] * len(plan),
        scratch_shapes=scratch,
        compiler_params=params(number),
        name="reduce_parts",
    )(*arrays)
    return [out.reshape(-1, out.shape[-1]) for out in outs]


def spread_kernel(pairs, pieces, in_ref, out_ref, local, s1, r1, s2, r2, s3, r3):
    outer, inner = spot("item")
    other, far = near("item")
    meet([other] + far)
    keep = pltpu.make_async_copy(in_ref, out_ref.at[outer, inner], local)
    keep.start()
    away, beside, onward = {}, [], []
    for p in range(pieces):
        for k in range(1, pairs):
            away[p, k] = send(
                in_ref.at[p],
                out_ref.at[outer, inner, p],
                (s1, r1),
                (k - 1) * pieces + p,
                far[k - 1],
            )
    for p in range(pieces):
        beside.append(send(in_ref.at[p], out_ref.at[outer, inner, p], (s2, r2), p, other))
    for p in range(pieces):
        for k in range(1, pairs):
            away[p, k].wait_recv()
            came = lax.rem(outer + pairs - k, pairs)
            onward.append(
                send(
                    out_ref.at[came, inner, p],
                    out_ref.at[came, inner, p],
                    (s3, r3),
                    (k - 1) * pieces + p,
                    other,
                )
            )
    keep.wait()
    for copy in beside + onward:
        copy.wait_recv()
    for copy in list(away.values()) + beside + onward:
        copy.wait_send()


def spread(array, number, pieces):
    pairs = lax.axis_size("item") // 2
    rows, width = array.shape
    others = max(pairs - 1, 1)
    out = pl.pallas_call(
        lambda *refs: spread_kernel(pairs, pieces, *refs),
        out_shape=jax.ShapeDtypeStruct((pairs, 2, pieces, rows // pieces, width), array.dtype),
        in_specs=[VMEM],
        out_specs=VMEM,
        scratch_shapes=[
            pltpu.SemaphoreType.DMA,
            *sem_pair(others * pieces),
            *sem_pair(pieces),
            *sem_pair(others * pieces),
        ],
        compiler_params=params(number),
        name="spread",
    )(array.reshape(pieces, rows // pieces, width))
    return out.reshape(-1, width)


def trade_kernel(
    pairs, users, split, in_ref, ids_ref, loss_ref, table_ref, sum_ref, blocks, names, losses, local,
    s0, r0, s1, r1, s2, r2, s3, r3, s4, r4, s5, r5,
):
    outer, inner = spot("item")
    me = lax.axis_index("dp")
    other, far = near("item")
    peers = [{"dp": lax.rem(me + k, users)} for k in range(1, users)]
    low = table_ref.shape[0] // split
    width = table_ref.shape[1]
    length = in_ref.shape[1]
    first = lax.axis_index("item") * table_ref.shape[0]
    meet([other] + far + peers)
    here = blocks.at[outer, inner]
    keep = pltpu.make_async_copy(in_ref.at[me], here.at[me], local)
    keep.start()
    names[me] = ids_ref[...]
    losses[me] = loss_ref[...]
    for k in range(1, users):
        send(ids_ref, names.at[me], (s4, r4), k, peers[k - 1])
        send(loss_ref, losses.at[me], (s5, r5), k, peers[k - 1])
    for k in range(1, users):
        send(in_ref.at[lax.rem(me + k, users)], here.at[me], (s0, r0), k, peers[k - 1])
    table_ref[...] = jnp.zeros_like(table_ref)

    def source(k):
        return lax.rem(me + users - k, users)

    def away(k, j):
        block = here.at[source(k)]
        return link(block, block, (s1, r1), (j - 1) * users + k, far[j - 1])

    def beside(k):
        block = here.at[source(k)]
        return link(block, block, (s2, r2), k, other)

    def onward(k, j):
        block = blocks.at[lax.rem(outer + pairs - j, pairs), inner, source(k)]
        return link(block, block, (s3, r3), (j - 1) * users + k, other)

    def add(k, at, place):
        user = source(k)
        ids = names[user, at * 2 + place] - first
        terms = blocks[at, place, user]
        row = ids & (low - 1) if split > 1 else ids
        hit = jnp.where(
            lax.broadcasted_iota(jnp.int32, (low, length), 0) == row, 1.0, 0.0
        ).astype(jnp.bfloat16)
        if split > 1:
            part = jnp.transpose(jnp.broadcast_to(ids // low, (width, length)))
            wide = terms.astype(jnp.float32)
            terms = jnp.concatenate(
                [jnp.where(part == h, wide, 0.0) for h in range(split)], axis=1
            ).astype(jnp.bfloat16)
        total = jnp.dot(hit, terms, preferred_element_type=jnp.float32)
        for h in range(split):
            table_ref[h * low : (h + 1) * low, :] += total[:, h * width : (h + 1) * width]

    def pass_on(k):
        for j in range(1, pairs):
            away(k, j).start()
        beside(k).start()
        add(k, outer, inner)

    keep.wait()
    pass_on(0)

    @pl.loop(1, users)
    def _(k):
        link(in_ref.at[me], here.at[me], (s0, r0), k, other).wait_recv()
        link(ids_ref, names.at[me], (s4, r4), k, other).wait_recv()
        pass_on(k)

    @pl.loop(0, users)
    def _(k):
        for j in range(1, pairs):
            away(k, j).wait_recv()
            onward(k, j).start()
            add(k, lax.rem(outer + pairs - j, pairs), inner)

    @pl.loop(0, users)
    def _(k):
        beside(k).wait_recv()
        add(k, outer, 1 - inner)
        for j in range(1, pairs):
            onward(k, j).wait_recv()
            add(k, lax.rem(outer + pairs - j, pairs), 1 - inner)

    for k in range(1, users):
        link(loss_ref, losses.at[me], (s5, r5), k, other).wait_recv()
    total = losses[0]
    for user in range(1, users):
        total = total + losses[user]
    sum_ref[...] = total

    @pl.loop(0, users)
    def _(k):
        beside(k).wait_send()
        for j in range(1, pairs):
            away(k, j).wait_send()
            onward(k, j).wait_send()

    @pl.loop(1, users)
    def _(k):
        link(in_ref.at[me], here.at[me], (s0, r0), k, other).wait_send()
        link(ids_ref, names.at[me], (s4, r4), k, other).wait_send()
        link(loss_ref, losses.at[me], (s5, r5), k, other).wait_send()


def trade(array, ids, loss, table_rows, number):
    pairs = lax.axis_size("item") // 2
    users, rows, width = array.shape
    others = max(pairs - 1, 1)
    split = 4 if width == 128 else 1
    return pl.pallas_call(
        lambda *refs: trade_kernel(pairs, users, split, *refs),
        out_shape=[
            jax.ShapeDtypeStruct((table_rows, width), jnp.float32),
            jax.ShapeDtypeStruct(loss.shape, jnp.float32),
        ],
        in_specs=[VMEM] * 3,
        out_specs=[VMEM] * 2,
        scratch_shapes=[
            pltpu.VMEM((pairs, 2, users, rows, width), array.dtype),
            pltpu.VMEM((users, *ids.shape), ids.dtype),
            pltpu.VMEM((users, *loss.shape), loss.dtype),
            pltpu.SemaphoreType.DMA,
            *sem_pair(users),
            *sem_pair(others * users),
            *sem_pair(users),
            *sem_pair(others * users),
            *sem_pair(users),
            *sem_pair(users),
        ],
        compiler_params=params(number),
        name="trade",
    )(array, ids, loss)


def on_device(table, w_uvqk, w_out, history, lengths, candidates, counts, actions, targets):
    rows_total = table.shape[0]
    width = table.shape[1]
    seq = history.shape[1]
    ncand = candidates.shape[1]
    parts = lax.axis_size("item")
    block = seq // parts
    owner = lax.axis_index("item")
    first_row = owner * rows_total
    heads_local = w_out.shape[0] // HD

    users = lax.axis_size("dp")
    ids = jnp.concatenate([history[0], candidates[0]]) - first_row
    hit = ids[:, None] == jnp.arange(rows_total, dtype=jnp.int32)[None, :]
    own = jnp.dot(hit.astype(jnp.bfloat16), table, preferred_element_type=jnp.float32)
    own = own.astype(jnp.bfloat16)
    rows, own_cand = lax.optimization_barrier((join(own[:seq], 0, 8), own[seq:]))
    rows_f = rows.astype(jnp.float32)
    cand_f = join_later(own_cand)
    crows = cand_f
    scale = lax.rsqrt(jnp.mean(rows_f * rows_f, axis=-1, keepdims=True) + 1e-06)
    normed_f = rows_f * scale
    normed = normed_f.astype(jnp.bfloat16)
    local_w = w_uvqk.reshape(width, -1)
    pre = jnp.dot(normed, local_w, preferred_element_type=jnp.float32)
    act = jax.nn.silu(pre).astype(jnp.bfloat16).reshape(seq, 4, heads_local, HD)
    gate_u, values, queries, keys = (act[:, 0], act[:, 1], act[:, 2], act[:, 3])
    length = lengths[0]
    places = jnp.arange(seq, dtype=jnp.int32)
    allowed = (places[None, :] <= places[:, None]) & (places[None, :] < length)
    weight = allowed.astype(jnp.float32) / length.astype(jnp.float32)
    logits = jnp.einsum("thd,shd->hts", queries, keys, preferred_element_type=jnp.float32) * HD ** (
        -0.5
    )
    attn = (jax.nn.silu(logits) * weight).astype(jnp.bfloat16)
    mixed = jnp.einsum("hts,shd->thd", attn, values, preferred_element_type=jnp.float32).reshape(
        seq, -1
    )
    sums, squares = tally(pair_sums(mixed, mixed * mixed), 1).reshape(2, seq)
    center = (sums / width)[:, None]
    rstd = lax.rsqrt(squares[:, None] / width - center * center + 1e-05)
    normo = (mixed - center) * rstd
    u_flat = gate_u.reshape(seq, -1).astype(jnp.float32)
    gated = (normo * u_flat).astype(jnp.bfloat16)
    out_part = jnp.dot(gated, w_out, preferred_element_type=jnp.float32).astype(jnp.bfloat16)
    out_rows = reduce_parts([("item", out_part.reshape(parts, block, width), 4)], 2)[0]
    begin = owner * block
    rows_block = lax.dynamic_slice_in_dim(rows_f, begin, block, 0)
    hidden = (rows_block + out_rows).astype(jnp.bfloat16)
    scores = jnp.einsum("td,cd->tc", hidden, crows, preferred_element_type=jnp.float32)
    slots = jnp.arange(ncand, dtype=jnp.int32)
    valid = slots[None, :] < counts[0]
    masked = jnp.where(valid, scores, -jnp.inf)
    top = jnp.max(masked, axis=-1, keepdims=True)
    expo = jnp.exp(masked - top)
    total = jnp.sum(expo, axis=-1, keepdims=True)
    lse = top[:, 0] + jnp.log(total[:, 0])
    soft = expo / total
    action_block = lax.dynamic_slice_in_dim(actions[0], begin, block, 0)
    target_block = lax.dynamic_slice_in_dim(targets[0], begin, block, 0)
    onehot = (slots[None, :] == action_block[:, None]).astype(jnp.float32)
    taken = jnp.sum(scores * onehot, axis=-1)
    block_places = begin + jnp.arange(block, dtype=jnp.int32)
    live = (block_places < length).astype(jnp.float32) / seq
    miss = taken - target_block
    loss_part = jnp.sum(live * (CQL_WEIGHT * (lse - taken) + 0.5 * miss * miss))
    dscore = (live[:, None] * (CQL_WEIGHT * soft + (miss - CQL_WEIGHT)[:, None] * onehot)).astype(
        jnp.bfloat16
    )
    dhidden = jnp.dot(dscore, crows, preferred_element_type=jnp.float32).astype(jnp.bfloat16)
    dcand_part = jnp.einsum("tc,td->cd", dscore, hidden, preferred_element_type=jnp.float32).astype(
        jnp.bfloat16
    )
    dh_full = spread(dhidden, 3, 4)
    dgated = jnp.einsum("td,ed->te", dh_full, w_out, preferred_element_type=jnp.float32)
    dw_out = jnp.einsum(
        "te,tdk->dek",
        gated,
        dh_full.reshape(seq, users, width // users),
        preferred_element_type=jnp.float32,
    ).astype(jnp.bfloat16)
    du = dgated * normo
    dnormo = dgated * u_flat
    sent = jnp.concatenate([pair_sums(dnormo, dnormo * normo), jnp.full((8, 128), loss_part)])
    sent = tally(sent, 4)
    first_sum, second_sum = sent[:-8].reshape(2, seq)
    first = (first_sum / width)[:, None]
    second = (second_sum / width)[:, None]
    dmixed = (
        (rstd * (dnormo - first - normo * second))
        .astype(jnp.bfloat16)
        .reshape(seq, heads_local, HD)
    )
    dattn = jnp.einsum("thd,shd->hts", dmixed, values, preferred_element_type=jnp.float32)
    dvalues = jnp.einsum("hts,thd->shd", attn, dmixed, preferred_element_type=jnp.float32)
    dlogits = (dattn * weight * silu_slope(logits) * HD ** (-0.5)).astype(jnp.bfloat16)
    dqueries = jnp.einsum("hts,shd->thd", dlogits, keys, preferred_element_type=jnp.float32)
    dkeys = jnp.einsum("hts,thd->shd", dlogits, queries, preferred_element_type=jnp.float32)
    dact = jnp.stack([du.reshape(seq, heads_local, HD), dvalues, dqueries, dkeys], axis=1).reshape(
        seq, -1
    )
    dpre = (dact * silu_slope(pre)).astype(jnp.bfloat16)
    dw_in = jnp.einsum("sd,sk->dk", normed, dpre, preferred_element_type=jnp.float32).astype(
        jnp.bfloat16
    )
    dnormed_part = jnp.einsum(
        "sk,dk->sd", dpre, local_w, preferred_element_type=jnp.float32
    ).astype(jnp.bfloat16)
    cblock = ncand // parts
    grad_proj = reduce_later(dw_out)
    dnormed, dcand, grad_in = reduce_parts(
        [
            ("item", dnormed_part.reshape(parts, block, width), 4),
            ("item", dcand_part.reshape(parts, cblock, width), 2),
            ("dp", dw_in.reshape(users, width // users, -1), 2),
        ],
        5,
    )
    grad_in = grad_in.reshape(width // users, 4, -1)
    scale_block = lax.dynamic_slice_in_dim(scale, begin, block, 0)
    normed_block = rows_block * scale_block
    drows = dhidden.astype(jnp.float32) + scale_block * (
        dnormed - normed_block * jnp.mean(dnormed * normed_block, axis=-1, keepdims=True)
    )
    terms = jnp.concatenate([drows, dcand]).astype(jnp.bfloat16)
    terms = terms.reshape(block + cblock, users, width // users).transpose(1, 0, 2)
    names = jnp.concatenate(
        [history[0].reshape(parts, 1, block), candidates[0].reshape(parts, 1, cblock)], axis=2
    )
    shard_grad, loss = trade(terms, names, sent[-8:], rows_total, 6)
    return (loss[0, 0], grad_in, grad_proj, shard_grad)


def solution(mesh):
    placed = (
        P("item", None),
        P(None, None, "item"),
        P("item", None),
        P("dp", None),
        P("dp"),
        P("dp", None),
        P("dp"),
        P("dp", None),
        P("dp", None),
    )
    return jax.shard_map(
        on_device,
        mesh=mesh,
        in_specs=placed,
        out_specs=(P(), P("dp", None, "item"), P("item", "dp"), P("item", "dp")),
        check_vma=False,
    )
```

```python
import jax
import jax.numpy as jnp
from jax import lax
from jax.experimental import pallas as pl
from jax.experimental.pallas import tpu as pltpu
from jax.sharding import PartitionSpec as P

HD = 128


CQL_WEIGHT = 0.5
MESH = pl.DeviceIdType.MESH
VMEM = pl.BlockSpec(memory_space=pltpu.VMEM)


def silu_slope(value):
    sigma = jax.nn.sigmoid(value)
    return sigma * (1.0 + value * (1.0 - sigma))


def spot(axis):
    me = lax.axis_index(axis)
    return me // 2, me % 2


def meet(peers):
    barrier = pltpu.get_barrier_semaphore()
    for peer in peers:
        pl.semaphore_signal(barrier, inc=1, device_id=peer, device_id_type=MESH)
    pl.semaphore_wait(barrier, len(peers))


def near(axis):
    pairs = lax.axis_size(axis) // 2
    outer, inner = spot(axis)
    other = {axis: outer * 2 + 1 - inner}
    far = [{axis: lax.rem(outer + k, pairs) * 2 + inner} for k in range(1, pairs)]
    return other, far


def link(src, dst, sems, index, peer):
    return pltpu.make_async_remote_copy(
        src_ref=src,
        dst_ref=dst,
        send_sem=sems[0].at[index],
        recv_sem=sems[1].at[index],
        device_id=peer,
        device_id_type=MESH,
    )


def send(*way):
    copy = link(*way)
    copy.start()
    return copy


def sem_pair(*shape):
    return [pltpu.SemaphoreType.DMA(shape), pltpu.SemaphoreType.DMA(shape)]


def params(number):
    return pltpu.CompilerParams(
        collective_id=number, has_side_effects=True, vmem_limit_bytes=40 * 1024 * 1024
    )


def join_kernel(pairs, pieces, in_ref, out_ref, got, mine, far_got, s1, r1, s2, r2, s3, r3):
    outer, inner = spot("item")
    other, far = near("item")
    meet([other] + far)
    first = [
        send(in_ref.at[1 - inner, p], got.at[p], (s1, r1), p, other) for p in range(pieces)
    ]
    second = []
    for p in range(pieces):
        first[p].wait_recv()
        mine[p] = in_ref[inner, p] + got[p]
        for k in range(1, pairs):
            second.append(
                send(mine.at[p], far_got.at[k - 1, p], (s2, r2), (k - 1) * pieces + p, far[k - 1])
            )
    third = []
    for p in range(pieces):
        total = mine[p]
        for k in range(1, pairs):
            second[p * (pairs - 1) + k - 1].wait_recv()
            total = total + far_got[k - 1, p]
        out_ref[inner, p] = total
        third.append(send(out_ref.at[inner, p], out_ref.at[inner, p], (s3, r3), p, other))
    for copy in third:
        copy.wait_recv()
    for copy in first + second + third:
        copy.wait_send()


def join(array, number, pieces):
    pairs = lax.axis_size("item") // 2
    rows, width = array.shape
    block = rows // 2 // pieces
    spread = (max(pairs - 1, 1) * pieces,)
    out = pl.pallas_call(
        lambda *refs: join_kernel(pairs, pieces, *refs),
        out_shape=jax.ShapeDtypeStruct((2, pieces, block, width), array.dtype),
        in_specs=[VMEM],
        out_specs=VMEM,
        scratch_shapes=[
            pltpu.VMEM((pieces, block, width), array.dtype),
            pltpu.VMEM((pieces, block, width), array.dtype),
            pltpu.VMEM((max(pairs - 1, 1), pieces, block, width), array.dtype),
            *sem_pair(pieces),
            *sem_pair(*spread),
            *sem_pair(pieces),
        ],
        compiler_params=params(number),
        name="join_rows",
    )(array.reshape(2, pieces, block, width))
    return out.reshape(rows, width)


def tally_kernel(count, in_ref, out_ref, got, ss, rs):
    me = lax.axis_index("item")
    peers = [{"item": lax.rem(me + k, count)} for k in range(1, count)]
    meet(peers)
    copies = [send(in_ref, got.at[me], (ss, rs), k, peer) for k, peer in enumerate(peers)]
    got[me] = in_ref[...]
    for copy in copies:
        copy.wait_recv()
    total = got[0]
    for source in range(1, count):
        total = total + got[source]
    out_ref[...] = total
    for copy in copies:
        copy.wait_send()


def tally(packed, number):
    count = lax.axis_size("item")
    return pl.pallas_call(
        lambda *refs: tally_kernel(count, *refs),
        out_shape=jax.ShapeDtypeStruct(packed.shape, packed.dtype),
        in_specs=[VMEM],
        out_specs=VMEM,
        scratch_shapes=[
            pltpu.VMEM((count, *packed.shape), packed.dtype),
            *sem_pair(count - 1),
        ],
        compiler_params=params(number),
        name="tally",
    )(packed)


def pair_sums(mixed, other):
    return jnp.stack([jnp.sum(mixed, axis=-1), jnp.sum(other, axis=-1)]).reshape(-1, 128)


def shift(array, axis, step):
    count = lax.axis_size(axis)
    if step == 0:
        moves = [(i, i ^ 1) for i in range(count)]
    else:
        moves = [(i, (i + 2 * step) % count) for i in range(count)]
    return lax.ppermute(array, axis, moves)


def join_later(array):
    pairs = lax.axis_size("item") // 2
    rows, width = array.shape
    _, inner = spot("item")
    halves = array.reshape(2, rows // 2, width)
    mine = lax.dynamic_index_in_dim(halves, inner, 0, False) + shift(
        lax.dynamic_index_in_dim(halves, 1 - inner, 0, False), "item", 0
    )
    total = mine
    for k in range(1, pairs):
        total = total + shift(mine, "item", k)
    other = shift(total, "item", 0)
    return jnp.where(inner == 0, jnp.stack([total, other]), jnp.stack([other, total])).reshape(
        rows, width
    )


def stages(axis, pairs, pieces, in_ref, got, mine, far_got, s1, r1, s2, r2):
    outer, inner = spot(axis)
    other, far = near(axis)
    first, second = {}, {}

    def start(p):
        for k in list(range(1, pairs)) + [0]:
            to = lax.rem(outer + k, pairs)
            first[p, k] = send(
                in_ref.at[to, 1 - inner, p], got.at[k, p], (s1, r1), k * pieces + p, other
            )

    def relay(p):
        for k in range(1, pairs):
            first[p, k].wait_recv()
            to = lax.rem(outer + k, pairs)
            mine[k - 1, p] = (
                in_ref[to, inner, p].astype(jnp.float32) + got[k, p].astype(jnp.float32)
            ).astype(jnp.bfloat16)
            second[p, k] = send(
                mine.at[k - 1, p], far_got.at[k - 1, p], (s2, r2), (k - 1) * pieces + p, far[k - 1]
            )

    def total(p):
        first[p, 0].wait_recv()
        result = in_ref[outer, inner, p].astype(jnp.float32) + got[0, p].astype(jnp.float32)
        for k in range(1, pairs):
            second[p, k].wait_recv()
            result = result + far_got[k - 1, p].astype(jnp.float32)
        return result

    def close():
        for copy in list(first.values()) + list(second.values()):
            copy.wait_send()

    return start, relay, total, close


def stage_scratch(pairs, pieces, block, width):
    others = max(pairs - 1, 1)
    return [
        pltpu.VMEM((pairs, pieces, block, width), jnp.bfloat16),
        pltpu.VMEM((others, pieces, block, width), jnp.bfloat16),
        pltpu.VMEM((others, pieces, block, width), jnp.bfloat16),
        *sem_pair(pairs * pieces),
        *sem_pair(others * pieces),
    ]


def middle_kernel(
    pairs, pieces, part_ref, rows_ref, crows_ref, valid_ref, action_ref, target_ref, live_ref,
    full_ref, dh_ref, hidden_ref, dscore_ref, loss_ref, *work,
):
    outer, inner = spot("item")
    other, far = near("item")
    meet([other] + far)
    start, relay, total, close = stages("item", pairs, pieces, part_ref, *work[:7])
    s1, r1, s2, r2, s3, r3 = work[7:]
    for p in range(pieces):
        start(p)
    for p in range(pieces):
        relay(p)
    away, beside, onward = {}, [], []

    def pass_on(p):
        for k in range(1, pairs):
            away[p, k].wait_recv()
            came = full_ref.at[lax.rem(outer + pairs - k, pairs), inner, p]
            onward.append(send(came, came, (s3, r3), (k - 1) * pieces + p, other))

    for p in range(pieces):
        hidden = (rows_ref[p].astype(jnp.float32) + total(p)).astype(jnp.bfloat16)
        hidden_ref[p] = hidden
        scores = lax.dot_general(
            hidden, crows_ref[...], (((1,), (1,)), ((), ())), preferred_element_type=jnp.float32
        )
        live = live_ref[p]
        masked = jnp.where(valid_ref[...] > 0, scores, -jnp.inf)
        top = jnp.max(masked, axis=-1, keepdims=True)
        expo = jnp.exp(masked - top)
        mass = jnp.sum(expo, axis=-1, keepdims=True)
        soft = expo / mass
        chosen = lax.broadcasted_iota(jnp.int32, scores.shape, 1) == action_ref[p]
        taken = jnp.sum(jnp.where(chosen, scores, 0.0), axis=-1, keepdims=True)
        miss = taken - target_ref[p]
        lse = top + jnp.log(mass)
        loss_ref[p] = live * (CQL_WEIGHT * (lse - taken) + 0.5 * miss * miss)
        dscore = live * (CQL_WEIGHT * soft + jnp.where(chosen, miss - CQL_WEIGHT, 0.0))
        dscore = dscore.astype(jnp.bfloat16)
        dscore_ref[p] = dscore
        dhidden = jnp.dot(dscore, crows_ref[...], preferred_element_type=jnp.float32)
        dhidden = dhidden.astype(jnp.bfloat16)
        dh_ref[p] = dhidden
        full_ref[outer, inner, p] = dhidden
        spot_there = full_ref.at[outer, inner, p]
        for k in range(1, pairs):
            away[p, k] = send(
                dh_ref.at[p], spot_there, (s1, r1), (k - 1) * pieces + p, far[k - 1]
            )
        beside.append(send(dh_ref.at[p], spot_there, (s2, r2), p, other))
        if p:
            pass_on(p - 1)
    pass_on(pieces - 1)
    for copy in beside + onward:
        copy.wait_recv()
    for copy in list(away.values()) + beside + onward:
        copy.wait_send()
    close()


def middle(part, rows, crows, valid, action, target, live, number, pieces):
    pairs = lax.axis_size("item") // 2
    block, width = rows.shape
    ncand = crows.shape[0]
    step = block // pieces
    others = max(pairs - 1, 1)
    full, dhidden, hidden, dscore, loss = pl.pallas_call(
        lambda *refs: middle_kernel(pairs, pieces, *refs),
        out_shape=[
            jax.ShapeDtypeStruct((pairs, 2, pieces, step, width), jnp.bfloat16),
            jax.ShapeDtypeStruct((pieces, step, width), jnp.bfloat16),
            jax.ShapeDtypeStruct((pieces, step, width), jnp.bfloat16),
            jax.ShapeDtypeStruct((pieces, step, ncand), jnp.bfloat16),
            jax.ShapeDtypeStruct((pieces, step, 1), jnp.float32),
        ],
        in_specs=[VMEM] * 7,
        out_specs=[VMEM] * 5,
        scratch_shapes=[
            *stage_scratch(pairs, pieces, step, width),
            *sem_pair(others * pieces),
            *sem_pair(pieces),
            *sem_pair(others * pieces),
        ],
        compiler_params=params(number),
        name="middle",
    )(
        part.reshape(pairs, 2, pieces, step, width),
        rows.reshape(pieces, step, width),
        crows,
        valid.reshape(1, ncand),
        action.reshape(pieces, step, 1),
        target.reshape(pieces, step, 1),
        live.reshape(pieces, step, 1),
    )
    return (
        full.reshape(-1, width),
        dhidden.reshape(block, width),
        hidden.reshape(block, width),
        dscore.reshape(block, ncand),
        jnp.sum(loss),
    )


def last_kernel(
    plan, users, split, dn_ref, dc_ref, dw_ref, do_ref, dh_ref, rows_ref, ids_ref, loss_ref,
    table_ref, sum_ref, win_ref, wout_ref, *work,
):
    made = [
        stages(*plan[i], ref, *work[7 * i : 7 * i + 7])
        for i, ref in enumerate((dn_ref, dc_ref, dw_ref, do_ref))
    ]
    in_ref, blocks, names, losses, local, s0, r0, s1, r1, s2, r2, s3, r3, s4, r4, s5, r5 = work[28:]
    pairs = plan[0][1]
    outer, inner = spot("item")
    me = lax.axis_index("dp")
    other, far = near("item")
    peers = [{"dp": lax.rem(me + k, users)} for k in range(1, users)]
    low = table_ref.shape[0] // split
    width = table_ref.shape[1]
    length = in_ref.shape[1]
    step = rows_ref.shape[1]
    cstep = dc_ref.shape[3]
    first = lax.axis_index("item") * table_ref.shape[0]
    meet([other] + far + peers)
    here = blocks.at[outer, inner]
    names[me] = ids_ref[...]
    losses[me] = loss_ref[...]
    for k in range(1, users):
        send(ids_ref, names.at[me], (s4, r4), k, peers[k - 1])
        send(loss_ref, losses.at[me], (s5, r5), k, peers[k - 1])
    rows_plan, cand_plan, win_plan, wout_plan = made
    for i in range(4):
        for p in range(plan[i][2]):
            made[i][0](p)
    for i in range(2):
        for p in range(plan[i][2]):
            made[i][1](p)
    table_ref[...] = jnp.zeros_like(table_ref)
    win_plan[1](0)
    for p in range(plan[0][2]):
        dnormed = rows_plan[2](p)
        rows = rows_ref[p].astype(jnp.float32)
        scale = lax.rsqrt(jnp.mean(rows * rows, axis=-1, keepdims=True) + 1e-06)
        normed = rows * scale
        drows = dh_ref[p].astype(jnp.float32) + scale * (
            dnormed - normed * jnp.mean(dnormed * normed, axis=-1, keepdims=True)
        )
        for user in range(users):
            in_ref[user, p * step : (p + 1) * step, :] = drows[
                :, user * width : (user + 1) * width
            ].astype(jnp.bfloat16)
    for p in range(plan[1][2]):
        dcand = cand_plan[2](p)
        begin = length - (plan[1][2] - p) * cstep
        for user in range(users):
            in_ref[user, begin : begin + cstep, :] = dcand[
                :, user * width : (user + 1) * width
            ].astype(jnp.bfloat16)
    keep = pltpu.make_async_copy(in_ref.at[me], here.at[me], local)
    keep.start()
    for k in range(1, users):
        send(in_ref.at[lax.rem(me + k, users)], here.at[me], (s0, r0), k, peers[k - 1])

    for p in range(1, plan[2][2]):
        win_plan[1](p)
    for p in range(plan[3][2]):
        wout_plan[1](p)

    def source(k):
        return lax.rem(me + users - k, users)

    def away(k, j):
        block = here.at[source(k)]
        return link(block, block, (s1, r1), (j - 1) * users + k, far[j - 1])

    def beside(k):
        block = here.at[source(k)]
        return link(block, block, (s2, r2), k, other)

    def onward(k, j):
        block = blocks.at[lax.rem(outer + pairs - j, pairs), inner, source(k)]
        return link(block, block, (s3, r3), (j - 1) * users + k, other)

    def add(k, at, place):
        user = source(k)
        ids = names[user, at * 2 + place] - first
        terms = blocks[at, place, user]
        row = ids & (low - 1) if split > 1 else ids
        hit = jnp.where(
            lax.broadcasted_iota(jnp.int32, (low, length), 0) == row, 1.0, 0.0
        ).astype(jnp.bfloat16)
        if split > 1:
            part = jnp.transpose(jnp.broadcast_to(ids // low, (width, length)))
            wide = terms.astype(jnp.float32)
            terms = jnp.concatenate(
                [jnp.where(part == h, wide, 0.0) for h in range(split)], axis=1
            ).astype(jnp.bfloat16)
        total = jnp.dot(hit, terms, preferred_element_type=jnp.float32)
        for h in range(split):
            table_ref[h * low : (h + 1) * low, :] += total[:, h * width : (h + 1) * width]

    def pass_on(k):
        for j in range(1, pairs):
            away(k, j).start()
        beside(k).start()
        add(k, outer, inner)

    keep.wait()
    pass_on(0)

    @pl.loop(1, users + 2)
    def _(k):
        @pl.when(k < users)
        def _():
            link(in_ref.at[me], here.at[me], (s0, r0), k, other).wait_recv()
            link(ids_ref, names.at[me], (s4, r4), k, other).wait_recv()
            pass_on(k)

        @pl.when(k < users + 1)
        def _():
            for j in range(1, pairs):
                away(k - 1, j).wait_recv()
                onward(k - 1, j).start()
                add(k - 1, lax.rem(outer + pairs - j, pairs), inner)

        @pl.when(k > 1)
        def _():
            beside(k - 2).wait_recv()
            add(k - 2, outer, 1 - inner)
            for j in range(1, pairs):
                onward(k - 2, j).wait_recv()
                add(k - 2, lax.rem(outer + pairs - j, pairs), 1 - inner)

    for p in range(plan[2][2]):
        win_ref[p] = win_plan[2](p)
    for p in range(plan[3][2]):
        wout_ref[p] = wout_plan[2](p)
    for one in made:
        one[3]()
    for k in range(1, users):
        link(loss_ref, losses.at[me], (s5, r5), k, other).wait_recv()
    total = losses[0]
    for user in range(1, users):
        total = total + losses[user]
    sum_ref[...] = total

    @pl.loop(0, users)
    def _(k):
        beside(k).wait_send()
        for j in range(1, pairs):
            away(k, j).wait_send()
            onward(k, j).wait_send()

    @pl.loop(1, users)
    def _(k):
        link(in_ref.at[me], here.at[me], (s0, r0), k, other).wait_send()
        link(ids_ref, names.at[me], (s4, r4), k, other).wait_send()
        link(loss_ref, losses.at[me], (s5, r5), k, other).wait_send()


def last(dnormed, dcand, dw_in, dw_out, dhidden, rows, ids, loss, table_rows, number):
    pairs = lax.axis_size("item") // 2
    users = lax.axis_size("dp")
    block, width = rows.shape
    cblock = dcand.shape[1]
    length, columns = block + cblock, width // users
    others = max(pairs - 1, 1)
    split = 4 if columns == 128 else 1
    plan, arrays, scratch = [], [], []
    for axis, array, pieces in (
        ("item", dnormed, 4),
        ("item", dcand, 2),
        ("dp", dw_in, 2),
        ("dp", dw_out, 1),
    ):
        half, step = array.shape[0] // 2, array.shape[1] // pieces
        plan.append((axis, half, pieces))
        arrays.append(array.reshape(half, 2, pieces, step, array.shape[2]))
        scratch += stage_scratch(half, pieces, step, array.shape[2])
    table, total, win, wout = pl.pallas_call(
        lambda *refs: last_kernel(plan, users, split, *refs),
        out_shape=[
            jax.ShapeDtypeStruct((table_rows, columns), jnp.float32),
            jax.ShapeDtypeStruct(loss.shape, jnp.float32),
            jax.ShapeDtypeStruct(arrays[2].shape[2:], jnp.float32),
            jax.ShapeDtypeStruct(arrays[3].shape[2:], jnp.float32),
        ],
        in_specs=[VMEM] * 8,
        out_specs=[VMEM] * 4,
        scratch_shapes=[
            *scratch,
            pltpu.VMEM((users, length, columns), jnp.bfloat16),
            pltpu.VMEM((pairs, 2, users, length, columns), jnp.bfloat16),
            pltpu.VMEM((users, *ids.shape), ids.dtype),
            pltpu.VMEM((users, *loss.shape), loss.dtype),
            pltpu.SemaphoreType.DMA,
            *sem_pair(users),
            *sem_pair(others * users),
            *sem_pair(users),
            *sem_pair(others * users),
            *sem_pair(users),
            *sem_pair(users),
        ],
        compiler_params=params(number),
        name="last",
    )(
        *arrays,
        dhidden.reshape(4, block // 4, width),
        rows.reshape(4, block // 4, width),
        ids,
        loss,
    )
    return table, total, win.reshape(-1, win.shape[-1]), wout.reshape(-1, wout.shape[-1])


def on_device(table, w_uvqk, w_out, history, lengths, candidates, counts, actions, targets):
    rows_total = table.shape[0]
    width = table.shape[1]
    seq = history.shape[1]
    ncand = candidates.shape[1]
    parts = lax.axis_size("item")
    block = seq // parts
    owner = lax.axis_index("item")
    first_row = owner * rows_total
    heads_local = w_out.shape[0] // HD

    users = lax.axis_size("dp")

    def pick(ids):
        hit = (ids - first_row)[:, None] == jnp.arange(rows_total, dtype=jnp.int32)[None, :]
        own = jnp.dot(hit.astype(jnp.bfloat16), table, preferred_element_type=jnp.float32)
        return own.astype(jnp.bfloat16)

    rows, own_cand = lax.optimization_barrier((join(pick(history[0]), 0, 8), pick(candidates[0])))
    rows_f = rows.astype(jnp.float32)
    cand_f = join_later(own_cand)
    crows = cand_f
    scale = lax.rsqrt(jnp.mean(rows_f * rows_f, axis=-1, keepdims=True) + 1e-06)
    normed_f = rows_f * scale
    normed = normed_f.astype(jnp.bfloat16)
    local_w = w_uvqk.reshape(width, -1)
    pre = jnp.dot(normed, local_w, preferred_element_type=jnp.float32)
    act = jax.nn.silu(pre).astype(jnp.bfloat16).reshape(seq, 4, heads_local, HD)
    gate_u, values, queries, keys = (act[:, 0], act[:, 1], act[:, 2], act[:, 3])
    length = lengths[0]
    places = jnp.arange(seq, dtype=jnp.int32)
    allowed = (places[None, :] <= places[:, None]) & (places[None, :] < length)
    weight = allowed.astype(jnp.float32) / length.astype(jnp.float32)
    logits = jnp.einsum("thd,shd->hts", queries, keys, preferred_element_type=jnp.float32) * HD ** (
        -0.5
    )
    attn = (jax.nn.silu(logits) * weight).astype(jnp.bfloat16)
    mixed = jnp.einsum("hts,shd->thd", attn, values, preferred_element_type=jnp.float32).reshape(
        seq, -1
    )
    sums, squares = tally(pair_sums(mixed, mixed * mixed), 1).reshape(2, seq)
    center = (sums / width)[:, None]
    rstd = lax.rsqrt(squares[:, None] / width - center * center + 1e-05)
    normo = (mixed - center) * rstd
    u_flat = gate_u.reshape(seq, -1).astype(jnp.float32)
    gated = (normo * u_flat).astype(jnp.bfloat16)
    out_part = jnp.dot(gated, w_out, preferred_element_type=jnp.float32).astype(jnp.bfloat16)
    begin = owner * block
    rows_block = lax.dynamic_slice_in_dim(rows, begin, block, 0)
    slots = jnp.arange(ncand, dtype=jnp.int32)
    valid = (slots < counts[0]).astype(jnp.int32)
    action_block = lax.dynamic_slice_in_dim(actions[0], begin, block, 0)
    target_block = lax.dynamic_slice_in_dim(targets[0], begin, block, 0)
    block_places = begin + jnp.arange(block, dtype=jnp.int32)
    live = (block_places < length).astype(jnp.float32) / seq
    dh_full, dhidden, hidden, dscore, loss_part = middle(
        out_part.reshape(parts, block, width),
        rows_block,
        crows,
        valid,
        action_block,
        target_block,
        live,
        2,
        4,
    )
    dcand_part = jnp.einsum("tc,td->cd", dscore, hidden, preferred_element_type=jnp.float32).astype(
        jnp.bfloat16
    )
    dgated = jnp.einsum("td,ed->te", dh_full, w_out, preferred_element_type=jnp.float32)
    dw_out = jnp.einsum(
        "te,tdk->dek",
        gated,
        dh_full.reshape(seq, users, width // users),
        preferred_element_type=jnp.float32,
    ).astype(jnp.bfloat16)
    du = dgated * normo
    dnormo = dgated * u_flat
    sent = jnp.concatenate([pair_sums(dnormo, dnormo * normo), jnp.full((8, 128), loss_part)])
    sent = tally(sent, 4)
    first_sum, second_sum = sent[:-8].reshape(2, seq)
    first = (first_sum / width)[:, None]
    second = (second_sum / width)[:, None]
    dmixed = (
        (rstd * (dnormo - first - normo * second))
        .astype(jnp.bfloat16)
        .reshape(seq, heads_local, HD)
    )
    dattn = jnp.einsum("thd,shd->hts", dmixed, values, preferred_element_type=jnp.float32)
    dvalues = jnp.einsum("hts,thd->shd", attn, dmixed, preferred_element_type=jnp.float32)
    dlogits = (dattn * weight * silu_slope(logits) * HD ** (-0.5)).astype(jnp.bfloat16)
    dqueries = jnp.einsum("hts,shd->thd", dlogits, keys, preferred_element_type=jnp.float32)
    dkeys = jnp.einsum("hts,thd->shd", dlogits, queries, preferred_element_type=jnp.float32)
    dact = jnp.stack([du.reshape(seq, heads_local, HD), dvalues, dqueries, dkeys], axis=1).reshape(
        seq, -1
    )
    dpre = (dact * silu_slope(pre)).astype(jnp.bfloat16)
    dw_in = jnp.einsum("sd,sk->dk", normed, dpre, preferred_element_type=jnp.float32).astype(
        jnp.bfloat16
    )
    dnormed_part = jnp.einsum(
        "sk,dk->sd", dpre, local_w, preferred_element_type=jnp.float32
    ).astype(jnp.bfloat16)
    cblock = ncand // parts
    names = jnp.concatenate(
        [history[0].reshape(parts, 1, block), candidates[0].reshape(parts, 1, cblock)], axis=2
    )
    shard_grad, loss, grad_in, grad_proj = last(
        dnormed_part.reshape(parts, block, width),
        dcand_part.reshape(parts, cblock, width),
        dw_in.reshape(users, width // users, -1),
        dw_out,
        dhidden,
        rows_block,
        names,
        sent[-8:],
        rows_total,
        6,
    )
    grad_in = grad_in.reshape(width // users, 4, -1)
    return (loss[0, 0], grad_in, grad_proj, shard_grad)


def solution(mesh):
    placed = (
        P("item", None),
        P(None, None, "item"),
        P("item", None),
        P("dp", None),
        P("dp"),
        P("dp", None),
        P("dp"),
        P("dp", None),
        P("dp", None),
    )
    return jax.shard_map(
        on_device,
        mesh=mesh,
        in_specs=placed,
        out_specs=(P(), P("dp", None, "item"), P("item", "dp"), P("item", "dp")),
        check_vma=False,
    )
```

```python
import jax
import jax.numpy as jnp
from jax import lax
from jax.experimental import pallas as pl
from jax.experimental.pallas import tpu as pltpu
from jax.sharding import PartitionSpec as P

HD = 128


CQL_WEIGHT = 0.5
MESH = pl.DeviceIdType.MESH
VMEM = pl.BlockSpec(memory_space=pltpu.VMEM)


def silu_slope(value):
    sigma = jax.nn.sigmoid(value)
    return sigma * (1.0 + value * (1.0 - sigma))


def spot(axis):
    me = lax.axis_index(axis)
    return me // 2, me % 2


def meet(peers):
    barrier = pltpu.get_barrier_semaphore()
    for peer in peers:
        pl.semaphore_signal(barrier, inc=1, device_id=peer, device_id_type=MESH)
    pl.semaphore_wait(barrier, len(peers))


def near(axis):
    pairs = lax.axis_size(axis) // 2
    outer, inner = spot(axis)
    other = {axis: outer * 2 + 1 - inner}
    far = [{axis: lax.rem(outer + k, pairs) * 2 + inner} for k in range(1, pairs)]
    return other, far


def link(src, dst, sems, index, peer):
    return pltpu.make_async_remote_copy(
        src_ref=src,
        dst_ref=dst,
        send_sem=sems[0].at[index],
        recv_sem=sems[1].at[index],
        device_id=peer,
        device_id_type=MESH,
    )


def send(*way):
    copy = link(*way)
    copy.start()
    return copy


def sem_pair(*shape):
    return [pltpu.SemaphoreType.DMA(shape), pltpu.SemaphoreType.DMA(shape)]


def params(number):
    return pltpu.CompilerParams(
        collective_id=number, has_side_effects=True, vmem_limit_bytes=40 * 1024 * 1024
    )


def join_kernel(
    pairs, counts, hist_ref, cand_ref, w_ref, rows_ref, crows_ref, normed_ref, pre_ref, act_ref,
    got, mine, far_got, s1, r1, s2, r2, s3, r3,
):
    outer, inner = spot("item")
    other, far = near("item")
    meet([other] + far)
    pieces = sum(counts)
    ins = [hist_ref.at[:, p] for p in range(counts[0])]
    ins += [cand_ref.at[:, p] for p in range(counts[1])]
    outs = [rows_ref.at[:, p] for p in range(counts[0])]
    outs += [crows_ref.at[:, p] for p in range(counts[1])]
    first = [send(ins[p].at[1 - inner], got.at[p], (s1, r1), p, other) for p in range(pieces)]
    second, third = {}, []
    for p in range(pieces):
        first[p].wait_recv()
        mine[p] = ins[p][inner] + got[p]
        for k in range(1, pairs):
            second[p, k] = send(
                mine.at[p], far_got.at[k - 1, p], (s2, r2), (k - 1) * pieces + p, far[k - 1]
            )

    def project(p):
        third[p].wait_recv()
        step = rows_ref.shape[2]
        rows = jnp.concatenate([rows_ref[inner, p], rows_ref[1 - inner, p]]).astype(jnp.float32)
        scale = lax.rsqrt(jnp.mean(rows * rows, axis=-1, keepdims=True) + 1e-06)
        normed = (rows * scale).astype(jnp.bfloat16)
        pre = jnp.dot(normed, w_ref[...], preferred_element_type=jnp.float32)
        act = (pre * jax.nn.sigmoid(pre)).astype(jnp.bfloat16)
        for place, begin in ((inner, 0), (1 - inner, step)):
            normed_ref[place, p] = normed[begin : begin + step]
            pre_ref[place, p] = pre[begin : begin + step]
            act_ref[place, p] = act[begin : begin + step]

    for p in range(pieces):
        total = mine[p]
        for k in range(1, pairs):
            second[p, k].wait_recv()
            total = total + far_got[k - 1, p]
        outs[p][inner] = total
        third.append(send(outs[p].at[inner], outs[p].at[inner], (s3, r3), p, other))
        if 0 < p <= counts[0]:
            project(p - 1)
    for p in range(counts[0], pieces):
        third[p].wait_recv()
    for copy in first + list(second.values()) + third:
        copy.wait_send()


def join(hist, cand, weights, number):
    pairs = lax.axis_size("item") // 2
    width = hist.shape[1]
    columns = weights.shape[1]
    step = 64
    counts = [hist.shape[0] // 2 // step, cand.shape[0] // 2 // step]
    pieces = sum(counts)
    others = max(pairs - 1, 1)
    tall = (2, counts[0], step)
    rows, crows, normed, pre, act = pl.pallas_call(
        lambda *refs: join_kernel(pairs, counts, *refs),
        out_shape=[
            jax.ShapeDtypeStruct((*tall, width), jnp.bfloat16),
            jax.ShapeDtypeStruct((2, counts[1], step, width), jnp.bfloat16),
            jax.ShapeDtypeStruct((*tall, width), jnp.bfloat16),
            jax.ShapeDtypeStruct((*tall, columns), jnp.float32),
            jax.ShapeDtypeStruct((*tall, columns), jnp.bfloat16),
        ],
        in_specs=[VMEM] * 3,
        out_specs=[VMEM] * 5,
        scratch_shapes=[
            pltpu.VMEM((pieces, step, width), jnp.bfloat16),
            pltpu.VMEM((pieces, step, width), jnp.bfloat16),
            pltpu.VMEM((others, pieces, step, width), jnp.bfloat16),
            *sem_pair(pieces),
            *sem_pair(others * pieces),
            *sem_pair(pieces),
        ],
        compiler_params=params(number),
        name="join_rows",
    )(hist.reshape(*tall, width), cand.reshape(2, counts[1], step, width), weights)
    return [part.reshape(-1, part.shape[-1]) for part in (rows, crows, normed, pre, act)]


def tally_kernel(count, in_ref, out_ref, got, ss, rs):
    me = lax.axis_index("item")
    peers = [{"item": lax.rem(me + k, count)} for k in range(1, count)]
    meet(peers)
    copies = [send(in_ref, got.at[me], (ss, rs), k, peer) for k, peer in enumerate(peers)]
    got[me] = in_ref[...]
    for copy in copies:
        copy.wait_recv()
    total = got[0]
    for source in range(1, count):
        total = total + got[source]
    out_ref[...] = total
    for copy in copies:
        copy.wait_send()


def tally(packed, number):
    count = lax.axis_size("item")
    return pl.pallas_call(
        lambda *refs: tally_kernel(count, *refs),
        out_shape=jax.ShapeDtypeStruct(packed.shape, packed.dtype),
        in_specs=[VMEM],
        out_specs=VMEM,
        scratch_shapes=[
            pltpu.VMEM((count, *packed.shape), packed.dtype),
            *sem_pair(count - 1),
        ],
        compiler_params=params(number),
        name="tally",
    )(packed)


def pair_sums(mixed, other):
    return jnp.stack([jnp.sum(mixed, axis=-1), jnp.sum(other, axis=-1)]).reshape(-1, 128)


def stages(axis, pairs, pieces, in_ref, got, mine, far_got, s1, r1, s2, r2):
    outer, inner = spot(axis)
    other, far = near(axis)
    first, second = {}, {}

    def start(p):
        for k in list(range(1, pairs)) + [0]:
            to = lax.rem(outer + k, pairs)
            first[p, k] = send(
                in_ref.at[to, 1 - inner, p], got.at[k, p], (s1, r1), k * pieces + p, other
            )

    def relay(p):
        for k in range(1, pairs):
            first[p, k].wait_recv()
            to = lax.rem(outer + k, pairs)
            mine[k - 1, p] = (
                in_ref[to, inner, p].astype(jnp.float32) + got[k, p].astype(jnp.float32)
            ).astype(jnp.bfloat16)
            second[p, k] = send(
                mine.at[k - 1, p], far_got.at[k - 1, p], (s2, r2), (k - 1) * pieces + p, far[k - 1]
            )

    def total(p):
        first[p, 0].wait_recv()
        result = in_ref[outer, inner, p].astype(jnp.float32) + got[0, p].astype(jnp.float32)
        for k in range(1, pairs):
            second[p, k].wait_recv()
            result = result + far_got[k - 1, p].astype(jnp.float32)
        return result

    def close():
        for copy in list(first.values()) + list(second.values()):
            copy.wait_send()

    return start, relay, total, close


def stage_scratch(pairs, pieces, block, width):
    others = max(pairs - 1, 1)
    return [
        pltpu.VMEM((pairs, pieces, block, width), jnp.bfloat16),
        pltpu.VMEM((others, pieces, block, width), jnp.bfloat16),
        pltpu.VMEM((others, pieces, block, width), jnp.bfloat16),
        *sem_pair(pairs * pieces),
        *sem_pair(others * pieces),
    ]


def middle_kernel(
    pairs, pieces, part_ref, rows_ref, crows_ref, valid_ref, action_ref, target_ref, live_ref,
    full_ref, dh_ref, hidden_ref, dscore_ref, loss_ref, *work,
):
    outer, inner = spot("item")
    other, far = near("item")
    meet([other] + far)
    start, relay, total, close = stages("item", pairs, pieces, part_ref, *work[:7])
    s1, r1, s2, r2, s3, r3 = work[7:]
    for p in range(pieces):
        start(p)
    for p in range(pieces):
        relay(p)
    away, beside, onward = {}, [], []

    def pass_on(p):
        for k in range(1, pairs):
            away[p, k].wait_recv()
            came = full_ref.at[lax.rem(outer + pairs - k, pairs), inner, p]
            onward.append(send(came, came, (s3, r3), (k - 1) * pieces + p, other))

    for p in range(pieces):
        hidden = (rows_ref[p].astype(jnp.float32) + total(p)).astype(jnp.bfloat16)
        hidden_ref[p] = hidden
        scores = lax.dot_general(
            hidden, crows_ref[...], (((1,), (1,)), ((), ())), preferred_element_type=jnp.float32
        )
        live = live_ref[p]
        masked = jnp.where(valid_ref[...] > 0, scores, -jnp.inf)
        top = jnp.max(masked, axis=-1, keepdims=True)
        expo = jnp.exp(masked - top)
        mass = jnp.sum(expo, axis=-1, keepdims=True)
        soft = expo / mass
        chosen = lax.broadcasted_iota(jnp.int32, scores.shape, 1) == action_ref[p]
        taken = jnp.sum(jnp.where(chosen, scores, 0.0), axis=-1, keepdims=True)
        miss = taken - target_ref[p]
        lse = top + jnp.log(mass)
        loss_ref[p] = live * (CQL_WEIGHT * (lse - taken) + 0.5 * miss * miss)
        dscore = live * (CQL_WEIGHT * soft + jnp.where(chosen, miss - CQL_WEIGHT, 0.0))
        dscore = dscore.astype(jnp.bfloat16)
        dscore_ref[p] = dscore
        dhidden = jnp.dot(dscore, crows_ref[...], preferred_element_type=jnp.float32)
        dhidden = dhidden.astype(jnp.bfloat16)
        dh_ref[p] = dhidden
        full_ref[outer, inner, p] = dhidden
        spot_there = full_ref.at[outer, inner, p]
        for k in range(1, pairs):
            away[p, k] = send(
                dh_ref.at[p], spot_there, (s1, r1), (k - 1) * pieces + p, far[k - 1]
            )
        beside.append(send(dh_ref.at[p], spot_there, (s2, r2), p, other))
        if p:
            pass_on(p - 1)
    pass_on(pieces - 1)
    for copy in beside + onward:
        copy.wait_recv()
    for copy in list(away.values()) + beside + onward:
        copy.wait_send()
    close()


def middle(part, rows, crows, valid, action, target, live, number, pieces):
    pairs = lax.axis_size("item") // 2
    block, width = rows.shape
    ncand = crows.shape[0]
    step = block // pieces
    others = max(pairs - 1, 1)
    full, dhidden, hidden, dscore, loss = pl.pallas_call(
        lambda *refs: middle_kernel(pairs, pieces, *refs),
        out_shape=[
            jax.ShapeDtypeStruct((pairs, 2, pieces, step, width), jnp.bfloat16),
            jax.ShapeDtypeStruct((pieces, step, width), jnp.bfloat16),
            jax.ShapeDtypeStruct((pieces, step, width), jnp.bfloat16),
            jax.ShapeDtypeStruct((pieces, step, ncand), jnp.bfloat16),
            jax.ShapeDtypeStruct((pieces, step, 1), jnp.float32),
        ],
        in_specs=[VMEM] * 7,
        out_specs=[VMEM] * 5,
        scratch_shapes=[
            *stage_scratch(pairs, pieces, step, width),
            *sem_pair(others * pieces),
            *sem_pair(pieces),
            *sem_pair(others * pieces),
        ],
        compiler_params=params(number),
        name="middle",
    )(
        part.reshape(pairs, 2, pieces, step, width),
        rows.reshape(pieces, step, width),
        crows,
        valid.reshape(1, ncand),
        action.reshape(pieces, step, 1),
        target.reshape(pieces, step, 1),
        live.reshape(pieces, step, 1),
    )
    return (
        full.reshape(-1, width),
        dhidden.reshape(block, width),
        hidden.reshape(block, width),
        dscore.reshape(block, ncand),
        jnp.sum(loss),
    )


def last_kernel(
    plan, users, split, dn_ref, dc_ref, dw_ref, do_ref, dh_ref, rows_ref, ids_ref, loss_ref,
    table_ref, sum_ref, win_ref, wout_ref, *work,
):
    made = [
        stages(*plan[i], ref, *work[7 * i : 7 * i + 7])
        for i, ref in enumerate((dn_ref, dc_ref, dw_ref, do_ref))
    ]
    in_ref, blocks, names, losses, local, s0, r0, s1, r1, s2, r2, s3, r3, s4, r4, s5, r5 = work[28:]
    pairs = plan[0][1]
    outer, inner = spot("item")
    me = lax.axis_index("dp")
    other, far = near("item")
    peers = [{"dp": lax.rem(me + k, users)} for k in range(1, users)]
    low = table_ref.shape[0] // split
    width = table_ref.shape[1]
    length = in_ref.shape[1]
    step = rows_ref.shape[1]
    cstep = dc_ref.shape[3]
    first = lax.axis_index("item") * table_ref.shape[0]
    meet([other] + far + peers)
    here = blocks.at[outer, inner]
    names[me] = ids_ref[...]
    losses[me] = loss_ref[...]
    for k in range(1, users):
        send(ids_ref, names.at[me], (s4, r4), k, peers[k - 1])
        send(loss_ref, losses.at[me], (s5, r5), k, peers[k - 1])
    rows_plan, cand_plan, win_plan, wout_plan = made
    for i in range(4):
        for p in range(plan[i][2]):
            made[i][0](p)
    for i in range(2):
        for p in range(plan[i][2]):
            made[i][1](p)
    table_ref[...] = jnp.zeros_like(table_ref)
    win_plan[1](0)
    for p in range(plan[0][2]):
        dnormed = rows_plan[2](p)
        rows = rows_ref[p].astype(jnp.float32)
        scale = lax.rsqrt(jnp.mean(rows * rows, axis=-1, keepdims=True) + 1e-06)
        normed = rows * scale
        drows = dh_ref[p].astype(jnp.float32) + scale * (
            dnormed - normed * jnp.mean(dnormed * normed, axis=-1, keepdims=True)
        )
        for user in range(users):
            in_ref[user, p * step : (p + 1) * step, :] = drows[
                :, user * width : (user + 1) * width
            ].astype(jnp.bfloat16)
    for p in range(plan[1][2]):
        dcand = cand_plan[2](p)
        begin = length - (plan[1][2] - p) * cstep
        for user in range(users):
            in_ref[user, begin : begin + cstep, :] = dcand[
                :, user * width : (user + 1) * width
            ].astype(jnp.bfloat16)
    keep = pltpu.make_async_copy(in_ref.at[me], here.at[me], local)
    keep.start()
    for k in range(1, users):
        send(in_ref.at[lax.rem(me + k, users)], here.at[me], (s0, r0), k, peers[k - 1])
    def source(k):
        return lax.rem(me + users - k, users)

    def away(k, j):
        block = here.at[source(k)]
        return link(block, block, (s1, r1), (j - 1) * users + k, far[j - 1])

    def beside(k):
        block = here.at[source(k)]
        return link(block, block, (s2, r2), k, other)

    def onward(k, j):
        block = blocks.at[lax.rem(outer + pairs - j, pairs), inner, source(k)]
        return link(block, block, (s3, r3), (j - 1) * users + k, other)

    def add(k, at, place):
        user = source(k)
        ids = names[user, at * 2 + place] - first
        terms = blocks[at, place, user]
        row = ids & (low - 1) if split > 1 else ids
        hit = jnp.where(
            lax.broadcasted_iota(jnp.int32, (low, length), 0) == row, 1.0, 0.0
        ).astype(jnp.bfloat16)
        if split > 1:
            part = jnp.transpose(jnp.broadcast_to(ids // low, (width, length)))
            wide = terms.astype(jnp.float32)
            terms = jnp.concatenate(
                [jnp.where(part == h, wide, 0.0) for h in range(split)], axis=1
            ).astype(jnp.bfloat16)
        total = jnp.dot(hit, terms, preferred_element_type=jnp.float32)
        for h in range(split):
            table_ref[h * low : (h + 1) * low, :] += total[:, h * width : (h + 1) * width]

    def pass_on(k):
        for j in range(1, pairs):
            away(k, j).start()
        beside(k).start()
        add(k, outer, inner)

    keep.wait()
    pass_on(0)

    def advance(k):
        @pl.when(k < users)
        def _():
            link(in_ref.at[me], here.at[me], (s0, r0), k, other).wait_recv()
            link(ids_ref, names.at[me], (s4, r4), k, other).wait_recv()
            pass_on(k)

        @pl.when(k < users + 1)
        def _():
            for j in range(1, pairs):
                away(k - 1, j).wait_recv()
                onward(k - 1, j).start()
                add(k - 1, lax.rem(outer + pairs - j, pairs), inner)

        @pl.when(k > 1)
        def _():
            beside(k - 2).wait_recv()
            add(k - 2, outer, 1 - inner)
            for j in range(1, pairs):
                onward(k - 2, j).wait_recv()
                add(k - 2, lax.rem(outer + pairs - j, pairs), 1 - inner)

    pl.loop(1, users // 2)(advance)
    for p in range(1, plan[2][2]):
        win_plan[1](p)
    for p in range(plan[3][2]):
        wout_plan[1](p)
    pl.loop(users // 2, users + 2)(advance)

    for p in range(plan[2][2]):
        win_ref[p] = win_plan[2](p)
    for p in range(plan[3][2]):
        wout_ref[p] = wout_plan[2](p)
    for one in made:
        one[3]()
    for k in range(1, users):
        link(loss_ref, losses.at[me], (s5, r5), k, other).wait_recv()
    total = losses[0]
    for user in range(1, users):
        total = total + losses[user]
    sum_ref[...] = total

    @pl.loop(0, users)
    def _(k):
        beside(k).wait_send()
        for j in range(1, pairs):
            away(k, j).wait_send()
            onward(k, j).wait_send()

    @pl.loop(1, users)
    def _(k):
        link(in_ref.at[me], here.at[me], (s0, r0), k, other).wait_send()
        link(ids_ref, names.at[me], (s4, r4), k, other).wait_send()
        link(loss_ref, losses.at[me], (s5, r5), k, other).wait_send()


def last(dnormed, dcand, dw_in, dw_out, dhidden, rows, ids, loss, table_rows, number):
    pairs = lax.axis_size("item") // 2
    users = lax.axis_size("dp")
    block, width = rows.shape
    cblock = dcand.shape[1]
    length, columns = block + cblock, width // users
    others = max(pairs - 1, 1)
    split = 4 if columns == 128 else 1
    plan, arrays, scratch = [], [], []
    for axis, array, pieces in (
        ("item", dnormed, 4),
        ("item", dcand, 2),
        ("dp", dw_in, 2),
        ("dp", dw_out, 1),
    ):
        half, step = array.shape[0] // 2, array.shape[1] // pieces
        plan.append((axis, half, pieces))
        arrays.append(array.reshape(half, 2, pieces, step, array.shape[2]))
        scratch += stage_scratch(half, pieces, step, array.shape[2])
    table, total, win, wout = pl.pallas_call(
        lambda *refs: last_kernel(plan, users, split, *refs),
        out_shape=[
            jax.ShapeDtypeStruct((table_rows, columns), jnp.float32),
            jax.ShapeDtypeStruct(loss.shape, jnp.float32),
            jax.ShapeDtypeStruct(arrays[2].shape[2:], jnp.float32),
            jax.ShapeDtypeStruct(arrays[3].shape[2:], jnp.float32),
        ],
        in_specs=[VMEM] * 8,
        out_specs=[VMEM] * 4,
        scratch_shapes=[
            *scratch,
            pltpu.VMEM((users, length, columns), jnp.bfloat16),
            pltpu.VMEM((pairs, 2, users, length, columns), jnp.bfloat16),
            pltpu.VMEM((users, *ids.shape), ids.dtype),
            pltpu.VMEM((users, *loss.shape), loss.dtype),
            pltpu.SemaphoreType.DMA,
            *sem_pair(users),
            *sem_pair(others * users),
            *sem_pair(users),
            *sem_pair(others * users),
            *sem_pair(users),
            *sem_pair(users),
        ],
        compiler_params=params(number),
        name="last",
    )(
        *arrays,
        dhidden.reshape(4, block // 4, width),
        rows.reshape(4, block // 4, width),
        ids,
        loss,
    )
    return table, total, win.reshape(-1, win.shape[-1]), wout.reshape(-1, wout.shape[-1])


def on_device(table, w_uvqk, w_out, history, lengths, candidates, counts, actions, targets):
    rows_total = table.shape[0]
    width = table.shape[1]
    seq = history.shape[1]
    ncand = candidates.shape[1]
    parts = lax.axis_size("item")
    block = seq // parts
    owner = lax.axis_index("item")
    first_row = owner * rows_total
    heads_local = w_out.shape[0] // HD

    users = lax.axis_size("dp")

    def pick(ids):
        hit = (ids - first_row)[:, None] == jnp.arange(rows_total, dtype=jnp.int32)[None, :]
        own = jnp.dot(hit.astype(jnp.bfloat16), table, preferred_element_type=jnp.float32)
        return own.astype(jnp.bfloat16)

    local_w = w_uvqk.reshape(width, -1)
    rows, crows, normed, pre, act = join(pick(history[0]), pick(candidates[0]), local_w, 0)
    act = act.reshape(seq, 4, heads_local, HD)
    gate_u, values, queries, keys = (act[:, 0], act[:, 1], act[:, 2], act[:, 3])
    length = lengths[0]
    places = jnp.arange(seq, dtype=jnp.int32)
    allowed = (places[None, :] <= places[:, None]) & (places[None, :] < length)
    weight = allowed.astype(jnp.float32) / length.astype(jnp.float32)
    logits = jnp.einsum("thd,shd->hts", queries, keys, preferred_element_type=jnp.float32) * HD ** (
        -0.5
    )
    attn = (jax.nn.silu(logits) * weight).astype(jnp.bfloat16)
    mixed = jnp.einsum("hts,shd->thd", attn, values, preferred_element_type=jnp.float32).reshape(
        seq, -1
    )
    sums, squares = tally(pair_sums(mixed, mixed * mixed), 1).reshape(2, seq)
    center = (sums / width)[:, None]
    rstd = lax.rsqrt(squares[:, None] / width - center * center + 1e-05)
    normo = (mixed - center) * rstd
    u_flat = gate_u.reshape(seq, -1).astype(jnp.float32)
    gated = (normo * u_flat).astype(jnp.bfloat16)
    out_part = jnp.dot(gated, w_out, preferred_element_type=jnp.float32).astype(jnp.bfloat16)
    begin = owner * block
    rows_block = lax.dynamic_slice_in_dim(rows, begin, block, 0)
    slots = jnp.arange(ncand, dtype=jnp.int32)
    valid = (slots < counts[0]).astype(jnp.int32)
    action_block = lax.dynamic_slice_in_dim(actions[0], begin, block, 0)
    target_block = lax.dynamic_slice_in_dim(targets[0], begin, block, 0)
    block_places = begin + jnp.arange(block, dtype=jnp.int32)
    live = (block_places < length).astype(jnp.float32) / seq
    dh_full, dhidden, hidden, dscore, loss_part = middle(
        out_part.reshape(parts, block, width),
        rows_block,
        crows,
        valid,
        action_block,
        target_block,
        live,
        2,
        4,
    )
    dcand_part = jnp.einsum("tc,td->cd", dscore, hidden, preferred_element_type=jnp.float32).astype(
        jnp.bfloat16
    )
    dgated = jnp.einsum("td,ed->te", dh_full, w_out, preferred_element_type=jnp.float32)
    dw_out = jnp.einsum(
        "te,tdk->dek",
        gated,
        dh_full.reshape(seq, users, width // users),
        preferred_element_type=jnp.float32,
    ).astype(jnp.bfloat16)
    du = dgated * normo
    dnormo = dgated * u_flat
    sent = jnp.concatenate([pair_sums(dnormo, dnormo * normo), jnp.full((8, 128), loss_part)])
    sent = tally(sent, 4)
    first_sum, second_sum = sent[:-8].reshape(2, seq)
    first = (first_sum / width)[:, None]
    second = (second_sum / width)[:, None]
    dmixed = (
        (rstd * (dnormo - first - normo * second))
        .astype(jnp.bfloat16)
        .reshape(seq, heads_local, HD)
    )
    dattn = jnp.einsum("thd,shd->hts", dmixed, values, preferred_element_type=jnp.float32)
    dvalues = jnp.einsum("hts,thd->shd", attn, dmixed, preferred_element_type=jnp.float32)
    dlogits = (dattn * weight * silu_slope(logits) * HD ** (-0.5)).astype(jnp.bfloat16)
    dqueries = jnp.einsum("hts,shd->thd", dlogits, keys, preferred_element_type=jnp.float32)
    dkeys = jnp.einsum("hts,thd->shd", dlogits, queries, preferred_element_type=jnp.float32)
    dact = jnp.stack([du.reshape(seq, heads_local, HD), dvalues, dqueries, dkeys], axis=1).reshape(
        seq, -1
    )
    dpre = (dact * silu_slope(pre)).astype(jnp.bfloat16)
    dw_in = jnp.einsum("sd,sk->dk", normed, dpre, preferred_element_type=jnp.float32).astype(
        jnp.bfloat16
    )
    dnormed_part = jnp.einsum(
        "sk,dk->sd", dpre, local_w, preferred_element_type=jnp.float32
    ).astype(jnp.bfloat16)
    cblock = ncand // parts
    names = jnp.concatenate(
        [history[0].reshape(parts, 1, block), candidates[0].reshape(parts, 1, cblock)], axis=2
    )
    shard_grad, loss, grad_in, grad_proj = last(
        dnormed_part.reshape(parts, block, width),
        dcand_part.reshape(parts, cblock, width),
        dw_in.reshape(users, width // users, -1),
        dw_out,
        dhidden,
        rows_block,
        names,
        sent[-8:],
        rows_total,
        6,
    )
    grad_in = grad_in.reshape(width // users, 4, -1)
    return (loss[0, 0], grad_in, grad_proj, shard_grad)


def solution(mesh):
    placed = (
        P("item", None),
        P(None, None, "item"),
        P("item", None),
        P("dp", None),
        P("dp"),
        P("dp", None),
        P("dp"),
        P("dp", None),
        P("dp", None),
    )
    return jax.shard_map(
        on_device,
        mesh=mesh,
        in_specs=placed,
        out_specs=(P(), P("dp", None, "item"), P("item", "dp"), P("item", "dp")),
        check_vma=False,
    )
```

```python
import jax
import jax.numpy as jnp
from jax import lax
from jax.experimental import pallas as pl
from jax.experimental.pallas import tpu as pltpu
from jax.sharding import PartitionSpec as P

HD = 128


CQL_WEIGHT = 0.5
MESH = pl.DeviceIdType.MESH
VMEM = pl.BlockSpec(memory_space=pltpu.VMEM)


def silu_slope(value):
    sigma = jax.nn.sigmoid(value)
    return sigma * (1.0 + value * (1.0 - sigma))


def spot(axis):
    me = lax.axis_index(axis)
    return me // 2, me % 2


def meet(peers):
    barrier = pltpu.get_barrier_semaphore()
    for peer in peers:
        pl.semaphore_signal(barrier, inc=1, device_id=peer, device_id_type=MESH)
    pl.semaphore_wait(barrier, len(peers))


def near(axis):
    pairs = lax.axis_size(axis) // 2
    outer, inner = spot(axis)
    other = {axis: outer * 2 + 1 - inner}
    far = [{axis: lax.rem(outer + k, pairs) * 2 + inner} for k in range(1, pairs)]
    return other, far


def link(src, dst, sems, index, peer):
    return pltpu.make_async_remote_copy(
        src_ref=src,
        dst_ref=dst,
        send_sem=sems[0].at[index],
        recv_sem=sems[1].at[index],
        device_id=peer,
        device_id_type=MESH,
    )


def send(*way):
    copy = link(*way)
    copy.start()
    return copy


def sem_pair(*shape):
    return [pltpu.SemaphoreType.DMA(shape), pltpu.SemaphoreType.DMA(shape)]


def params(number):
    return pltpu.CompilerParams(
        collective_id=number, has_side_effects=True, vmem_limit_bytes=40 * 1024 * 1024
    )


def join_kernel(
    pairs, counts, hist_ref, cand_ref, w_ref, rows_ref, crows_ref, normed_ref, slope_ref, act_ref,
    got, mine, far_got, s1, r1, s2, r2, s3, r3,
):
    outer, inner = spot("item")
    other, far = near("item")
    meet([other] + far)
    pieces = sum(counts)
    ins = [hist_ref.at[:, p] for p in range(counts[0])]
    ins += [cand_ref.at[:, p] for p in range(counts[1])]
    outs = [rows_ref.at[:, p] for p in range(counts[0])]
    outs += [crows_ref.at[:, p] for p in range(counts[1])]
    first = [send(ins[p].at[1 - inner], got.at[p], (s1, r1), p, other) for p in range(pieces)]
    second, third = {}, []
    for p in range(pieces):
        first[p].wait_recv()
        mine[p] = ins[p][inner] + got[p]
        for k in range(1, pairs):
            second[p, k] = send(
                mine.at[p], far_got.at[k - 1, p], (s2, r2), (k - 1) * pieces + p, far[k - 1]
            )

    def project(p):
        third[p].wait_recv()
        step = rows_ref.shape[2]
        rows = jnp.concatenate([rows_ref[inner, p], rows_ref[1 - inner, p]]).astype(jnp.float32)
        scale = lax.rsqrt(jnp.mean(rows * rows, axis=-1, keepdims=True) + 1e-06)
        normed = (rows * scale).astype(jnp.bfloat16)
        pre = jnp.dot(normed, w_ref[...], preferred_element_type=jnp.float32)
        sigma = jax.nn.sigmoid(pre)
        act = (pre * sigma).astype(jnp.bfloat16)
        slope = (sigma * (1.0 + pre * (1.0 - sigma))).astype(jnp.bfloat16)
        for place, begin in ((inner, 0), (1 - inner, step)):
            normed_ref[place, p] = normed[begin : begin + step]
            slope_ref[place, p] = slope[begin : begin + step]
            act_ref[place, p] = act[begin : begin + step]

    for p in range(pieces):
        total = mine[p]
        for k in range(1, pairs):
            second[p, k].wait_recv()
            total = total + far_got[k - 1, p]
        outs[p][inner] = total
        third.append(send(outs[p].at[inner], outs[p].at[inner], (s3, r3), p, other))
        if 0 < p <= counts[0]:
            project(p - 1)
    for p in range(counts[0], pieces):
        third[p].wait_recv()
    for copy in first + list(second.values()) + third:
        copy.wait_send()


def join(hist, cand, weights, number):
    pairs = lax.axis_size("item") // 2
    width = hist.shape[1]
    columns = weights.shape[1]
    step = 64
    counts = [hist.shape[0] // 2 // step, cand.shape[0] // 2 // step]
    pieces = sum(counts)
    others = max(pairs - 1, 1)
    tall = (2, counts[0], step)
    rows, crows, normed, slope, act = pl.pallas_call(
        lambda *refs: join_kernel(pairs, counts, *refs),
        out_shape=[
            jax.ShapeDtypeStruct((*tall, width), jnp.bfloat16),
            jax.ShapeDtypeStruct((2, counts[1], step, width), jnp.bfloat16),
            jax.ShapeDtypeStruct((*tall, width), jnp.bfloat16),
            jax.ShapeDtypeStruct((*tall, columns), jnp.bfloat16),
            jax.ShapeDtypeStruct((*tall, columns), jnp.bfloat16),
        ],
        in_specs=[VMEM] * 3,
        out_specs=[VMEM] * 5,
        scratch_shapes=[
            pltpu.VMEM((pieces, step, width), jnp.bfloat16),
            pltpu.VMEM((pieces, step, width), jnp.bfloat16),
            pltpu.VMEM((others, pieces, step, width), jnp.bfloat16),
            *sem_pair(pieces),
            *sem_pair(others * pieces),
            *sem_pair(pieces),
        ],
        compiler_params=params(number),
        name="join_rows",
    )(hist.reshape(*tall, width), cand.reshape(2, counts[1], step, width), weights)
    return [part.reshape(-1, part.shape[-1]) for part in (rows, crows, normed, slope, act)]


def tally_kernel(count, in_ref, out_ref, got, ss, rs):
    me = lax.axis_index("item")
    peers = [{"item": lax.rem(me + k, count)} for k in range(1, count)]
    meet(peers)
    copies = [send(in_ref, got.at[me], (ss, rs), k, peer) for k, peer in enumerate(peers)]
    got[me] = in_ref[...]
    for copy in copies:
        copy.wait_recv()
    total = got[0]
    for source in range(1, count):
        total = total + got[source]
    out_ref[...] = total
    for copy in copies:
        copy.wait_send()


def tally(packed, number):
    count = lax.axis_size("item")
    return pl.pallas_call(
        lambda *refs: tally_kernel(count, *refs),
        out_shape=jax.ShapeDtypeStruct(packed.shape, packed.dtype),
        in_specs=[VMEM],
        out_specs=VMEM,
        scratch_shapes=[
            pltpu.VMEM((count, *packed.shape), packed.dtype),
            *sem_pair(count - 1),
        ],
        compiler_params=params(number),
        name="tally",
    )(packed)


def pair_sums(mixed, other):
    return jnp.stack([jnp.sum(mixed, axis=-1), jnp.sum(other, axis=-1)]).reshape(-1, 128)


def stages(axis, pairs, pieces, in_ref, got, mine, far_got, s1, r1, s2, r2):
    outer, inner = spot(axis)
    other, far = near(axis)
    first, second = {}, {}

    def start(p):
        for k in list(range(1, pairs)) + [0]:
            to = lax.rem(outer + k, pairs)
            first[p, k] = send(
                in_ref.at[to, 1 - inner, p], got.at[k, p], (s1, r1), k * pieces + p, other
            )

    def relay(p):
        for k in range(1, pairs):
            first[p, k].wait_recv()
            to = lax.rem(outer + k, pairs)
            mine[k - 1, p] = (
                in_ref[to, inner, p].astype(jnp.float32) + got[k, p].astype(jnp.float32)
            ).astype(jnp.bfloat16)
            second[p, k] = send(
                mine.at[k - 1, p], far_got.at[k - 1, p], (s2, r2), (k - 1) * pieces + p, far[k - 1]
            )

    def total(p):
        first[p, 0].wait_recv()
        result = in_ref[outer, inner, p].astype(jnp.float32) + got[0, p].astype(jnp.float32)
        for k in range(1, pairs):
            second[p, k].wait_recv()
            result = result + far_got[k - 1, p].astype(jnp.float32)
        return result

    def close():
        for copy in list(first.values()) + list(second.values()):
            copy.wait_send()

    return start, relay, total, close


def stage_scratch(pairs, pieces, block, width):
    others = max(pairs - 1, 1)
    return [
        pltpu.VMEM((pairs, pieces, block, width), jnp.bfloat16),
        pltpu.VMEM((others, pieces, block, width), jnp.bfloat16),
        pltpu.VMEM((others, pieces, block, width), jnp.bfloat16),
        *sem_pair(pairs * pieces),
        *sem_pair(others * pieces),
    ]


def middle_kernel(
    pairs, pieces, part_ref, rows_ref, crows_ref, valid_ref, action_ref, target_ref, live_ref,
    full_ref, dh_ref, hidden_ref, dscore_ref, loss_ref, *work,
):
    outer, inner = spot("item")
    other, far = near("item")
    meet([other] + far)
    start, relay, total, close = stages("item", pairs, pieces, part_ref, *work[:7])
    s1, r1, s2, r2, s3, r3 = work[7:]
    for p in range(pieces):
        start(p)
    for p in range(pieces):
        relay(p)
    away, beside, onward = {}, [], []

    def pass_on(p):
        for k in range(1, pairs):
            away[p, k].wait_recv()
            came = full_ref.at[lax.rem(outer + pairs - k, pairs), inner, p]
            onward.append(send(came, came, (s3, r3), (k - 1) * pieces + p, other))

    for p in range(pieces):
        hidden = (rows_ref[p].astype(jnp.float32) + total(p)).astype(jnp.bfloat16)
        hidden_ref[p] = hidden
        scores = lax.dot_general(
            hidden, crows_ref[...], (((1,), (1,)), ((), ())), preferred_element_type=jnp.float32
        )
        live = live_ref[p]
        masked = jnp.where(valid_ref[...] > 0, scores, -jnp.inf)
        top = jnp.max(masked, axis=-1, keepdims=True)
        expo = jnp.exp(masked - top)
        mass = jnp.sum(expo, axis=-1, keepdims=True)
        soft = expo / mass
        chosen = lax.broadcasted_iota(jnp.int32, scores.shape, 1) == action_ref[p]
        taken = jnp.sum(jnp.where(chosen, scores, 0.0), axis=-1, keepdims=True)
        miss = taken - target_ref[p]
        lse = top + jnp.log(mass)
        loss_ref[p] = live * (CQL_WEIGHT * (lse - taken) + 0.5 * miss * miss)
        dscore = live * (CQL_WEIGHT * soft + jnp.where(chosen, miss - CQL_WEIGHT, 0.0))
        dscore = dscore.astype(jnp.bfloat16)
        dscore_ref[p] = dscore
        dhidden = jnp.dot(dscore, crows_ref[...], preferred_element_type=jnp.float32)
        dhidden = dhidden.astype(jnp.bfloat16)
        dh_ref[p] = dhidden
        full_ref[outer, inner, p] = dhidden
        spot_there = full_ref.at[outer, inner, p]
        for k in range(1, pairs):
            away[p, k] = send(
                dh_ref.at[p], spot_there, (s1, r1), (k - 1) * pieces + p, far[k - 1]
            )
        beside.append(send(dh_ref.at[p], spot_there, (s2, r2), p, other))
        if p:
            pass_on(p - 1)
    pass_on(pieces - 1)
    for copy in beside + onward:
        copy.wait_recv()
    for copy in list(away.values()) + beside + onward:
        copy.wait_send()
    close()


def middle(part, rows, crows, valid, action, target, live, number, pieces):
    pairs = lax.axis_size("item") // 2
    block, width = rows.shape
    ncand = crows.shape[0]
    step = block // pieces
    others = max(pairs - 1, 1)
    full, dhidden, hidden, dscore, loss = pl.pallas_call(
        lambda *refs: middle_kernel(pairs, pieces, *refs),
        out_shape=[
            jax.ShapeDtypeStruct((pairs, 2, pieces, step, width), jnp.bfloat16),
            jax.ShapeDtypeStruct((pieces, step, width), jnp.bfloat16),
            jax.ShapeDtypeStruct((pieces, step, width), jnp.bfloat16),
            jax.ShapeDtypeStruct((pieces, step, ncand), jnp.bfloat16),
            jax.ShapeDtypeStruct((pieces, step, 1), jnp.float32),
        ],
        in_specs=[VMEM] * 7,
        out_specs=[VMEM] * 5,
        scratch_shapes=[
            *stage_scratch(pairs, pieces, step, width),
            *sem_pair(others * pieces),
            *sem_pair(pieces),
            *sem_pair(others * pieces),
        ],
        compiler_params=params(number),
        name="middle",
    )(
        part.reshape(pairs, 2, pieces, step, width),
        rows.reshape(pieces, step, width),
        crows,
        valid.reshape(1, ncand),
        action.reshape(pieces, step, 1),
        target.reshape(pieces, step, 1),
        live.reshape(pieces, step, 1),
    )
    return (
        full.reshape(-1, width),
        dhidden.reshape(block, width),
        hidden.reshape(block, width),
        dscore.reshape(block, ncand),
        jnp.sum(loss),
    )


def last_kernel(
    plan, users, split, dn_ref, dc_ref, dw_ref, do_ref, dh_ref, rows_ref, ids_ref, loss_ref,
    table_ref, sum_ref, win_ref, wout_ref, *work,
):
    made = [
        stages(*plan[i], ref, *work[7 * i : 7 * i + 7])
        for i, ref in enumerate((dn_ref, dc_ref, dw_ref, do_ref))
    ]
    in_ref, blocks, names, losses, local, s0, r0, s1, r1, s2, r2, s3, r3, s4, r4, s5, r5 = work[28:]
    pairs = plan[0][1]
    outer, inner = spot("item")
    me = lax.axis_index("dp")
    other, far = near("item")
    peers = [{"dp": lax.rem(me + k, users)} for k in range(1, users)]
    low = table_ref.shape[0] // split
    width = table_ref.shape[1]
    length = in_ref.shape[1]
    step = rows_ref.shape[1]
    cstep = dc_ref.shape[3]
    first = lax.axis_index("item") * table_ref.shape[0]
    meet([other] + far + peers)
    here = blocks.at[outer, inner]
    names[me] = ids_ref[...]
    losses[me] = loss_ref[...]
    for k in range(1, users):
        send(ids_ref, names.at[me], (s4, r4), k, peers[k - 1])
        send(loss_ref, losses.at[me], (s5, r5), k, peers[k - 1])
    rows_plan, cand_plan, win_plan, wout_plan = made
    for i in range(4):
        for p in range(plan[i][2]):
            made[i][0](p)
    for i in range(2):
        for p in range(plan[i][2]):
            made[i][1](p)
    table_ref[...] = jnp.zeros_like(table_ref)
    win_plan[1](0)
    for p in range(plan[0][2]):
        dnormed = rows_plan[2](p)
        rows = rows_ref[p].astype(jnp.float32)
        scale = lax.rsqrt(jnp.mean(rows * rows, axis=-1, keepdims=True) + 1e-06)
        normed = rows * scale
        drows = dh_ref[p].astype(jnp.float32) + scale * (
            dnormed - normed * jnp.mean(dnormed * normed, axis=-1, keepdims=True)
        )
        for user in range(users):
            in_ref[user, p * step : (p + 1) * step, :] = drows[
                :, user * width : (user + 1) * width
            ].astype(jnp.bfloat16)
    for p in range(plan[1][2]):
        dcand = cand_plan[2](p)
        begin = length - (plan[1][2] - p) * cstep
        for user in range(users):
            in_ref[user, begin : begin + cstep, :] = dcand[
                :, user * width : (user + 1) * width
            ].astype(jnp.bfloat16)
    keep = pltpu.make_async_copy(in_ref.at[me], here.at[me], local)
    keep.start()
    for k in range(1, users):
        send(in_ref.at[lax.rem(me + k, users)], here.at[me], (s0, r0), k, peers[k - 1])
    def source(k):
        return lax.rem(me + users - k, users)

    def away(k, j):
        block = here.at[source(k)]
        return link(block, block, (s1, r1), (j - 1) * users + k, far[j - 1])

    def beside(k):
        block = here.at[source(k)]
        return link(block, block, (s2, r2), k, other)

    def onward(k, j):
        block = blocks.at[lax.rem(outer + pairs - j, pairs), inner, source(k)]
        return link(block, block, (s3, r3), (j - 1) * users + k, other)

    def add(k, at, place):
        user = source(k)
        ids = names[user, at * 2 + place] - first
        terms = blocks[at, place, user]
        row = ids & (low - 1) if split > 1 else ids
        hit = jnp.where(
            lax.broadcasted_iota(jnp.int32, (low, length), 0) == row, 1.0, 0.0
        ).astype(jnp.bfloat16)
        if split > 1:
            part = jnp.transpose(jnp.broadcast_to(ids // low, (width, length)))
            wide = terms.astype(jnp.float32)
            terms = jnp.concatenate(
                [jnp.where(part == h, wide, 0.0) for h in range(split)], axis=1
            ).astype(jnp.bfloat16)
        total = jnp.dot(hit, terms, preferred_element_type=jnp.float32)
        for h in range(split):
            table_ref[h * low : (h + 1) * low, :] += total[:, h * width : (h + 1) * width]

    def pass_on(k):
        for j in range(1, pairs):
            away(k, j).start()
        beside(k).start()
        add(k, outer, inner)

    keep.wait()
    pass_on(0)

    def advance(k):
        @pl.when(k < users)
        def _():
            link(in_ref.at[me], here.at[me], (s0, r0), k, other).wait_recv()
            link(ids_ref, names.at[me], (s4, r4), k, other).wait_recv()
            pass_on(k)

        @pl.when(k < users + 1)
        def _():
            for j in range(1, pairs):
                away(k - 1, j).wait_recv()
                onward(k - 1, j).start()
                add(k - 1, lax.rem(outer + pairs - j, pairs), inner)

        @pl.when(k > 1)
        def _():
            beside(k - 2).wait_recv()
            add(k - 2, outer, 1 - inner)
            for j in range(1, pairs):
                onward(k - 2, j).wait_recv()
                add(k - 2, lax.rem(outer + pairs - j, pairs), 1 - inner)

    pl.loop(1, users // 2)(advance)
    for p in range(1, plan[2][2]):
        win_plan[1](p)
    for p in range(plan[3][2]):
        wout_plan[1](p)
    pl.loop(users // 2, users + 2)(advance)

    for p in range(plan[2][2]):
        win_ref[p] = win_plan[2](p)
    for p in range(plan[3][2]):
        wout_ref[p] = wout_plan[2](p)
    for one in made:
        one[3]()
    for k in range(1, users):
        link(loss_ref, losses.at[me], (s5, r5), k, other).wait_recv()
    total = losses[0]
    for user in range(1, users):
        total = total + losses[user]
    sum_ref[...] = total

    @pl.loop(0, users)
    def _(k):
        beside(k).wait_send()
        for j in range(1, pairs):
            away(k, j).wait_send()
            onward(k, j).wait_send()

    @pl.loop(1, users)
    def _(k):
        link(in_ref.at[me], here.at[me], (s0, r0), k, other).wait_send()
        link(ids_ref, names.at[me], (s4, r4), k, other).wait_send()
        link(loss_ref, losses.at[me], (s5, r5), k, other).wait_send()


def last(dnormed, dcand, dw_in, dw_out, dhidden, rows, ids, loss, table_rows, number):
    pairs = lax.axis_size("item") // 2
    users = lax.axis_size("dp")
    block, width = rows.shape
    cblock = dcand.shape[1]
    length, columns = block + cblock, width // users
    others = max(pairs - 1, 1)
    split = 4 if columns == 128 else 1
    plan, arrays, scratch = [], [], []
    for axis, array, pieces in (
        ("item", dnormed, 4),
        ("item", dcand, 2),
        ("dp", dw_in, 2),
        ("dp", dw_out, 1),
    ):
        half, step = array.shape[0] // 2, array.shape[1] // pieces
        plan.append((axis, half, pieces))
        arrays.append(array.reshape(half, 2, pieces, step, array.shape[2]))
        scratch += stage_scratch(half, pieces, step, array.shape[2])
    table, total, win, wout = pl.pallas_call(
        lambda *refs: last_kernel(plan, users, split, *refs),
        out_shape=[
            jax.ShapeDtypeStruct((table_rows, columns), jnp.float32),
            jax.ShapeDtypeStruct(loss.shape, jnp.float32),
            jax.ShapeDtypeStruct(arrays[2].shape[2:], jnp.float32),
            jax.ShapeDtypeStruct(arrays[3].shape[2:], jnp.float32),
        ],
        in_specs=[VMEM] * 8,
        out_specs=[VMEM] * 4,
        scratch_shapes=[
            *scratch,
            pltpu.VMEM((users, length, columns), jnp.bfloat16),
            pltpu.VMEM((pairs, 2, users, length, columns), jnp.bfloat16),
            pltpu.VMEM((users, *ids.shape), ids.dtype),
            pltpu.VMEM((users, *loss.shape), loss.dtype),
            pltpu.SemaphoreType.DMA,
            *sem_pair(users),
            *sem_pair(others * users),
            *sem_pair(users),
            *sem_pair(others * users),
            *sem_pair(users),
            *sem_pair(users),
        ],
        compiler_params=params(number),
        name="last",
    )(
        *arrays,
        dhidden.reshape(4, block // 4, width),
        rows.reshape(4, block // 4, width),
        ids,
        loss,
    )
    return table, total, win.reshape(-1, win.shape[-1]), wout.reshape(-1, wout.shape[-1])


def on_device(table, w_uvqk, w_out, history, lengths, candidates, counts, actions, targets):
    rows_total = table.shape[0]
    width = table.shape[1]
    seq = history.shape[1]
    ncand = candidates.shape[1]
    parts = lax.axis_size("item")
    block = seq // parts
    owner = lax.axis_index("item")
    first_row = owner * rows_total
    heads_local = w_out.shape[0] // HD

    users = lax.axis_size("dp")

    def pick(ids):
        hit = (ids - first_row)[:, None] == jnp.arange(rows_total, dtype=jnp.int32)[None, :]
        own = jnp.dot(hit.astype(jnp.bfloat16), table, preferred_element_type=jnp.float32)
        return own.astype(jnp.bfloat16)

    local_w = w_uvqk.reshape(width, -1)
    rows, crows, normed, slope, act = join(pick(history[0]), pick(candidates[0]), local_w, 0)
    group = heads_local * HD
    gate_u, values, queries, keys = (
        act[:, i * group : (i + 1) * group].reshape(seq, heads_local, HD) for i in range(4)
    )
    length = lengths[0]
    places = jnp.arange(seq, dtype=jnp.int32)
    allowed = (places[None, :] <= places[:, None]) & (places[None, :] < length)
    weight = allowed.astype(jnp.float32) / length.astype(jnp.float32)
    logits = jnp.einsum("thd,shd->hts", queries, keys, preferred_element_type=jnp.float32) * HD ** (
        -0.5
    )
    attn = (jax.nn.silu(logits) * weight).astype(jnp.bfloat16)
    mixed = jnp.einsum("hts,shd->thd", attn, values, preferred_element_type=jnp.float32).reshape(
        seq, -1
    )
    sums, squares = tally(pair_sums(mixed, mixed * mixed), 1).reshape(2, seq)
    center = (sums / width)[:, None]
    rstd = lax.rsqrt(squares[:, None] / width - center * center + 1e-05)
    normo = (mixed - center) * rstd
    u_flat = gate_u.reshape(seq, -1).astype(jnp.float32)
    gated = (normo * u_flat).astype(jnp.bfloat16)
    out_part = jnp.dot(gated, w_out, preferred_element_type=jnp.float32).astype(jnp.bfloat16)
    begin = owner * block
    rows_block = lax.dynamic_slice_in_dim(rows, begin, block, 0)
    slots = jnp.arange(ncand, dtype=jnp.int32)
    valid = (slots < counts[0]).astype(jnp.int32)
    action_block = lax.dynamic_slice_in_dim(actions[0], begin, block, 0)
    target_block = lax.dynamic_slice_in_dim(targets[0], begin, block, 0)
    block_places = begin + jnp.arange(block, dtype=jnp.int32)
    live = (block_places < length).astype(jnp.float32) / seq
    dh_full, dhidden, hidden, dscore, loss_part = middle(
        out_part.reshape(parts, block, width),
        rows_block,
        crows,
        valid,
        action_block,
        target_block,
        live,
        2,
        4,
    )
    dcand_part = jnp.einsum("tc,td->cd", dscore, hidden, preferred_element_type=jnp.float32).astype(
        jnp.bfloat16
    )
    dgated = jnp.einsum("td,ed->te", dh_full, w_out, preferred_element_type=jnp.float32)
    dw_out = jnp.einsum(
        "te,tdk->dek",
        gated,
        dh_full.reshape(seq, users, width // users),
        preferred_element_type=jnp.float32,
    ).astype(jnp.bfloat16)
    du = dgated * normo
    dnormo = dgated * u_flat
    sent = jnp.concatenate([pair_sums(dnormo, dnormo * normo), jnp.full((8, 128), loss_part)])
    sent = tally(sent, 4)
    first_sum, second_sum = sent[:-8].reshape(2, seq)
    first = (first_sum / width)[:, None]
    second = (second_sum / width)[:, None]
    dmixed = (
        (rstd * (dnormo - first - normo * second))
        .astype(jnp.bfloat16)
        .reshape(seq, heads_local, HD)
    )
    dattn = jnp.einsum("thd,shd->hts", dmixed, values, preferred_element_type=jnp.float32)
    dvalues = jnp.einsum("hts,thd->shd", attn, dmixed, preferred_element_type=jnp.float32)
    dlogits = (dattn * weight * silu_slope(logits) * HD ** (-0.5)).astype(jnp.bfloat16)
    dqueries = jnp.einsum("hts,shd->thd", dlogits, keys, preferred_element_type=jnp.float32)
    dkeys = jnp.einsum("hts,thd->shd", dlogits, queries, preferred_element_type=jnp.float32)
    dact = [du, dvalues.reshape(seq, -1), dqueries.reshape(seq, -1), dkeys.reshape(seq, -1)]
    dpre = jnp.concatenate(
        [
            (part * slope[:, i * group : (i + 1) * group].astype(jnp.float32)).astype(jnp.bfloat16)
            for i, part in enumerate(dact)
        ],
        axis=1,
    )
    dw_in = jnp.einsum("sd,sk->dk", normed, dpre, preferred_element_type=jnp.float32).astype(
        jnp.bfloat16
    )
    dnormed_part = jnp.einsum(
        "sk,dk->sd", dpre, local_w, preferred_element_type=jnp.float32
    ).astype(jnp.bfloat16)
    cblock = ncand // parts
    names = jnp.concatenate(
        [history[0].reshape(parts, 1, block), candidates[0].reshape(parts, 1, cblock)], axis=2
    )
    shard_grad, loss, grad_in, grad_proj = last(
        dnormed_part.reshape(parts, block, width),
        dcand_part.reshape(parts, cblock, width),
        dw_in.reshape(users, width // users, -1),
        dw_out,
        dhidden,
        rows_block,
        names,
        sent[-8:],
        rows_total,
        6,
    )
    grad_in = grad_in.reshape(width // users, 4, -1)
    return (loss[0, 0], grad_in, grad_proj, shard_grad)


def solution(mesh):
    placed = (
        P("item", None),
        P(None, None, "item"),
        P("item", None),
        P("dp", None),
        P("dp"),
        P("dp", None),
        P("dp"),
        P("dp", None),
        P("dp", None),
    )
    return jax.shard_map(
        on_device,
        mesh=mesh,
        in_specs=placed,
        out_specs=(P(), P("dp", None, "item"), P("item", "dp"), P("item", "dp")),
        check_vma=False,
    )
```
